512 devices in a mesh: blk: 128 (over y, z, core), pair: 4 (over x).
Axes of the slice: x: 4, y: 8, z: 8, core: 2. Of those that a mesh axis runs over, the one named last changes fastest.
Arguments:
- raw: bfloat16 [128, 128, 16384], P('blk', 'pair'), may hold values from -6 to 6
- pair_list: int32 [768, 2], replicated, may hold values from 0 to 127, as said below
Outputs:
- stack: float32 [128, 128, 16, 512], P('blk', 'pair')
The draws below stay inside these ranges and needn't reach their ends.
Inputs may be any that keep to these rules, and one draw needn't show every extreme that they name: `pair_list`: each row (i, j) names two blocks with 1 <= j - i <= 8 and j < 128; no pair appears twice.
All inputs are finite; a program needn't handle non-finite values.
Results may differ from the reference program's by a relative error of at most 0.0062.
Values may be sent and summed in bfloat16 or wider, within the bound.
A program may use at most 64 MiB of HBM per device.

```python
import math
import jax
import jax.numpy as jnp
from jax import lax

SPLIT = 128
NT = 16384
CH_BLK = 128
NBAND = 20
REACH = 8
LAG = 512
NBLK = 128
CHANNELS = 16384
NPAIRS = 768


def draw_pair_list(key, part):
    key = jax.random.fold_in(key, 7)
    key_weight, key_jitter = jax.random.split(key)
    slot_count = NBLK * REACH
    position = jnp.arange(slot_count, dtype=jnp.int32)
    leading = position // REACH
    offset = position % REACH + 1
    weight = jax.random.randint(key_weight, (NBLK,), 0, 4, dtype=jnp.int32)
    jitter = jax.random.randint(key_jitter, (slot_count,), 0, 4096, dtype=jnp.int32)
    ranking = (weight[leading] * 4096 + jitter) * slot_count + position
    ranking = jnp.where(leading + offset < NBLK, ranking, -1)
    chosen = lax.top_k(ranking, NPAIRS)[1]
    return jnp.stack([leading[chosen], leading[chosen] + offset[chosen]], axis=1).astype(jnp.int32)


def level_of(rng, extent, cuts, smallest, top_value):
    def one(dim, shards_of):
        draws = jax.random.uniform(jax.random.fold_in(jax.random.fold_in(rng, 6), dim), (shards_of,), jnp.float32, smallest / len(cuts), top_value / len(cuts))
        return jnp.repeat(jnp.exp(draws), extent[dim] // shards_of).reshape((-1,) + (1,) * (len(extent) - dim - 1))

    gain = one(*cuts[0])
    for cut in cuts[1:]:
        gain = gain * one(*cut)
    return gain


def normal_values(own_key, extent, spread, bound, shards=(), kind=jnp.bfloat16):
    result = jax.random.normal(own_key, extent, jnp.float32) * spread
    if len(shards) > 0:
        result = level_of(own_key, extent, shards, -0.22, 0.18) * result
    return jnp.clip(result, min=-bound, max=bound).astype(kind)


def setup_inputs(seed: int = 0) -> dict:
    splits = jax.random.split(jax.random.key(seed), 3)
    return {
        "raw": normal_values(splits[0], (SPLIT, SPLIT, CHANNELS), 1.0, 6.0, ((0, 128), (1, 4))),
        "pair_list": draw_pair_list(jax.random.fold_in(splits[2], 71), 0),
    }


EPSILON = 1e-06

def dft_tables():
    index = jnp.arange(SPLIT, dtype=jnp.int32)
    angle = (index[:, None] * index[None, :] % SPLIT).astype(jnp.float32) * (2.0 * math.pi / SPLIT)
    return (jnp.cos(angle).astype(jnp.bfloat16), jnp.sin(angle).astype(jnp.bfloat16))

def phase_tables(left, right):
    angle = (left * right % NT).astype(jnp.float32) * (2.0 * math.pi / NT)
    return (jnp.cos(angle), jnp.sin(angle))

def reference(raw, pair_list):
    cos_table, sin_table = dft_tables()
    cos_wide = cos_table.astype(jnp.float32)
    sin_wide = sin_table.astype(jnp.float32)
    samples = jnp.arange(SPLIT, dtype=jnp.int32)
    band_index = jnp.arange(NBAND, dtype=jnp.int32)
    bin_grid = samples[:, None] + SPLIT * band_index[None, :]
    twiddle_cos, twiddle_sin = phase_tables(bin_grid[:, :, None], samples[None, None, :])
    highest = lax.Precision.HIGHEST

    def spectrum(block_index):
        record = lax.dynamic_slice_in_dim(raw, block_index * CH_BLK, CH_BLK, 2).astype(jnp.float32)
        first_re = jnp.einsum('kn,nmc->kmc', cos_wide, record, precision=highest)
        first_im = -jnp.einsum('kn,nmc->kmc', sin_wide, record, precision=highest)
        spec_re = jnp.einsum('abn,anc->abc', twiddle_cos, first_re, precision=highest) + jnp.einsum('abn,anc->abc', twiddle_sin, first_im, precision=highest)
        spec_im = jnp.einsum('abn,anc->abc', twiddle_cos, first_im, precision=highest) - jnp.einsum('abn,anc->abc', twiddle_sin, first_re, precision=highest)
        band_power = lax.optimization_barrier(jnp.sum(spec_re * spec_re + spec_im * spec_im, axis=0))
        whitening = lax.rsqrt(band_power / SPLIT + EPSILON)[None]
        white = jnp.stack([(spec_re * whitening).astype(jnp.bfloat16), (spec_im * whitening).astype(jnp.bfloat16)])
        return jnp.transpose(white, (0, 3, 1, 2)).reshape(2, CH_BLK, SPLIT * NBAND)
    spectra = lax.map(spectrum, jnp.arange(NBLK, dtype=jnp.int32))
    bin_flat = bin_grid.reshape(-1)
    lag_index = jnp.arange(LAG, dtype=jnp.int32)
    lag_cos, lag_sin = phase_tables(bin_flat[:, None], lag_index[None, :])
    lag_cos = lag_cos.astype(jnp.bfloat16)
    lag_sin = lag_sin.astype(jnp.bfloat16)
    inv_root = 1.0 / math.sqrt(NBAND * SPLIT)

    def add_pair(stack, pair):
        first_block = pair[0].astype(jnp.int32)
        second_block = pair[1].astype(jnp.int32)
        own_f32 = spectra[first_block].astype(jnp.float32)
        other_f32 = spectra[second_block].astype(jnp.float32)
        cross_re = (own_f32[0] * other_f32[0] + own_f32[1] * other_f32[1]).astype(jnp.bfloat16)
        cross_im = (own_f32[1] * other_f32[0] - own_f32[0] * other_f32[1]).astype(jnp.bfloat16)
        even_part = jnp.dot(cross_re, lag_cos, preferred_element_type=jnp.float32)
        odd_part = jnp.dot(cross_im, lag_sin, preferred_element_type=jnp.float32)
        causal = (even_part - odd_part) * inv_root
        far_half = (even_part + odd_part) * inv_root
        distance = second_block - first_block
        zero_index = jnp.zeros((), jnp.int32)
        stack = lax.dynamic_update_slice(stack, causal[None, :, None, :], (first_block, zero_index, distance - 1, zero_index))
        stack = lax.dynamic_update_slice(stack, far_half[None, :, None, :], (second_block, zero_index, REACH + distance - 1, zero_index))
        return (stack, None)
    initial = jnp.zeros((NBLK, CH_BLK, 2 * REACH, LAG), jnp.float32)
    stack, _ = lax.scan(add_pair, initial, pair_list)
    return stack
```

```python
import math

import jax
import jax.numpy as jnp
import ml_dtypes
import numpy as np
from jax import lax
from jax.experimental import pallas as pl
from jax.experimental.pallas import tpu as pltpu
from jax.sharding import PartitionSpec as P

SPLIT = 128
NT = SPLIT * SPLIT
NBAND = 20
REACH = 8
LAG = 512
ROW = 16
NROW = 8
PAIR = 4
HALF = SPLIT // 2
BINS = 2 * NBAND
NBINS = HALF * BINS
EPSILON = 1e-06
VMEM = 56 * 1024 * 1024
MESH = pl.DeviceIdType.MESH
bf16 = jnp.bfloat16
f32 = jnp.float32


def first_table():
    angle = 2.0 * np.pi / SPLIT * (np.outer(np.arange(SPLIT), np.arange(SPLIT)) % SPLIT)
    table = np.concatenate([np.cos(angle[: HALF + 1]), -np.sin(angle[1:HALF])])
    return table.astype(ml_dtypes.bfloat16)


def slot_bins():
    slot = np.arange(HALF)[:, None, None]
    band = np.arange(NBAND)[None, :, None]
    mirror = np.where(slot == 0, HALF, SPLIT - slot)
    low = np.where(np.arange(2)[None, None, :] == 0, slot, mirror)
    return (low + SPLIT * band).reshape(HALF, BINS)


def angle_of(product):
    return 2.0 * np.pi / NT * (product % NT)


def second_tables():
    bins = slot_bins()
    worker, h = np.arange(PAIR)[:, None], np.arange(8)[None, :]
    sample = (32 * worker + h).reshape(-1)
    phi = angle_of(bins[:, :, None] * sample)
    cos, sin = np.cos(phi), np.sin(phi)
    sign = np.where(np.arange(BINS) % 2 == 0, 1.0, -1.0)[None, :, None]
    re = np.concatenate([cos, sign * sin], 2)
    im = np.concatenate([-sin, sign * cos], 2)
    zero = np.zeros_like(cos[0])
    even = (np.arange(BINS) % 2 == 0)[:, None]
    re[0] = np.concatenate([np.where(even, cos[0], zero), np.where(even, zero, cos[0])], 1)
    im[0] = np.concatenate([np.where(even, -sin[0], zero), np.where(even, zero, -sin[0])], 1)
    full = np.concatenate([re, im], 1)
    high = full.astype(ml_dtypes.bfloat16)
    low = (full - high.astype(np.float64)).astype(ml_dtypes.bfloat16)
    weights = np.concatenate([high, high, low], 2)
    quarter = np.repeat(8 * np.arange(4), 32)
    psi = angle_of(bins[:, :, None] * quarter)
    return weights, np.cos(psi).astype(np.float32), np.sin(psi).astype(np.float32)


def lag_tables():
    angle = angle_of(np.arange(LAG)[:, None] * slot_bins().reshape(-1)[None, :])
    return np.cos(angle).astype(ml_dtypes.bfloat16), np.sin(angle).astype(ml_dtypes.bfloat16)


def order_table():
    table = np.zeros((512, 512), ml_dtypes.bfloat16)
    for block in range(ROW):
        for e in range(2):
            for d in range(REACH):
                row = block * 32 + e * 16 + d
                table[row, 32 * d + 2 * block + e] = 1
                table[row + 8, 256 + 32 * d + 2 * ((block - d - 1) % ROW) + e] = 1
    return table


def swap_bits(tiles, bits):
    lane = lax.broadcasted_iota(jnp.int32, tiles[0].shape, 1)
    tiles = list(tiles)
    for bit, shift in bits:
        low_half = (lane & shift) == 0
        for low in range(len(tiles)):
            if low & bit:
                continue
            a, b = tiles[low], tiles[low | bit]
            tiles[low] = jnp.where(low_half, a, pltpu.roll(b, shift, 1))
            tiles[low | bit] = jnp.where(low_half, pltpu.roll(a, 128 - shift, 1), b)
    return tiles


STRIDE = 37


def peer(me, step):
    place = lax.rem(step * STRIDE, 128)
    row = lax.rem(me // 16 + place // 16, 8)
    chip = lax.rem((me // 2) % 8 + (place // 2) % 8, 8)
    core = lax.rem(me % 2 + place % 2, 2)
    return row * 16 + chip * 2 + core


def regroup_kernel(raw_ref, out_ref, sent, landed, quarters, send_sem, recv_sem, xs_sem, xr_sem, own_sem):
    me, worker = lax.axis_index("blk"), lax.axis_index("pair")
    barrier = pltpu.get_barrier_semaphore()

    def greet(step, carry):
        pl.semaphore_signal(barrier, inc=1, device_id=(peer(me, step), worker), device_id_type=MESH)
        return carry

    lax.fori_loop(1, 128, greet, 0)
    for step in range(1, PAIR):
        pl.semaphore_signal(
            barrier, inc=1, device_id=(me, lax.rem(worker + step, PAIR)), device_id_type=MESH
        )

    def spread(index, carry):
        row, half = index // 2, index % 2
        rows = pl.ds(pl.multiple_of(half * 16, 16), 16)
        tiles = []
        for block in range(ROW):
            at = pl.multiple_of(row * 2048 + block * 128, 128)
            tiles.append(raw_ref[0, rows, pl.ds(at, 128)].astype(f32))
        tiles = swap_bits(tiles, [(1, 2), (2, 4), (4, 8), (8, 16)])
        for block in range(ROW):
            sent[row * 16 + block, rows, :] = tiles[block].astype(bf16)
        return carry

    lax.fori_loop(0, 16, spread, 0)
    pl.semaphore_wait(barrier, 127 + PAIR - 1)

    def send(step, carry):
        there = peer(me, step)
        pltpu.make_async_remote_copy(
            src_ref=sent.at[there],
            dst_ref=landed.at[me],
            send_sem=send_sem,
            recv_sem=recv_sem,
            device_id=(there, worker),
            device_id_type=MESH,
        ).start()
        return carry

    lax.fori_loop(1, 128, send, 0)
    landed[me] = sent[me]
    many = pltpu.make_async_remote_copy(
        src_ref=sent.at[pl.ds(0, 127)],
        dst_ref=landed.at[pl.ds(0, 127)],
        send_sem=send_sem,
        recv_sem=recv_sem,
        device_id=(me, lax.rem(worker + 1, PAIR)),
        device_id_type=MESH,
    )
    many.wait_recv()

    def quarter(index, carry):
        parts = []
        for k in range(2):
            block = landed[index * 2 + k].astype(f32)
            tiles = [block[8 * q : 8 * q + 8] for q in range(4)]
            parts.append(swap_bits(tiles, [(1, 32), (2, 64)]))
        for w in range(PAIR):
            both = jnp.concatenate([parts[0][w], parts[1][w]], 0).astype(bf16)
            quarters[w, pl.ds(pl.multiple_of(index * 16, 16), 16), :] = both
        return carry

    lax.fori_loop(0, 64, quarter, 0)
    copies = []
    for step in range(1, PAIR):
        there = lax.rem(worker + step, PAIR)
        copy = pltpu.make_async_remote_copy(
            src_ref=quarters.at[there],
            dst_ref=out_ref.at[worker],
            send_sem=xs_sem.at[step],
            recv_sem=xr_sem.at[step],
            device_id=(me, there),
            device_id_type=MESH,
        )
        copy.start()
        copies.append(copy)
    own = pltpu.make_async_copy(quarters.at[worker], out_ref.at[worker], own_sem)
    own.start()
    many.wait_send()
    own.wait()
    for copy in copies:
        copy.wait()


def regroup(raw):
    return pl.pallas_call(
        regroup_kernel,
        name="regroup",
        out_shape=jax.ShapeDtypeStruct((PAIR, 1024, 128), bf16),
        in_specs=[pl.BlockSpec(memory_space=pltpu.VMEM)],
        out_specs=pl.BlockSpec(memory_space=pl.ANY),
        scratch_shapes=[
            pltpu.VMEM((128, 32, 128), bf16),
            pltpu.VMEM((128, 32, 128), bf16),
            pltpu.VMEM((PAIR, 1024, 128), bf16),
            pltpu.SemaphoreType.DMA,
            pltpu.SemaphoreType.DMA,
            pltpu.SemaphoreType.DMA((PAIR,)),
            pltpu.SemaphoreType.DMA((PAIR,)),
            pltpu.SemaphoreType.DMA,
        ],
        compiler_params=pltpu.CompilerParams(
            collective_id=0, has_side_effects=True, vmem_limit_bytes=VMEM
        ),
    )(raw)


def spectrum_kernel(z_ref, t_ref, w_ref, c_ref, s_ref, re_ref, im_ref, edge_ref, wide, first, spec_re, spec_im):
    for w in range(PAIR):
        wide[pl.ds(1024 * w, 1024), :] = z_ref[w].astype(f32)
    table = t_ref[...]

    def transform(index, carry):
        at = (index // 4) * 1024 + (index % 4) * 2
        pair = [wide[pl.ds(at + k, 128, stride=8), :].astype(bf16) for k in range(2)]
        got = jnp.dot(table, jnp.concatenate(pair, 1), preferred_element_type=f32)
        first[index * 2] = got[:, :128]
        first[index * 2 + 1] = got[:, 128:]
        return carry

    lax.fori_loop(0, 16, transform, 0, unroll=2)
    flat = first.reshape(32 * 128, 128)

    def bands(slot, power):
        a = flat[pl.ds(slot, 32, stride=128), :]
        b = flat[pl.ds(slot + HALF, 32, stride=128), :]
        both = jnp.concatenate([a, b], 0)
        high = both.astype(bf16)
        low = (both - high.astype(f32)).astype(bf16)
        got = jnp.dot(
            w_ref[slot], jnp.concatenate([high, low, high], 0), preferred_element_type=f32
        )
        part_re, part_im = got[:BINS], got[BINS:]
        cos, sin = c_ref[slot], s_ref[slot]
        re = part_re * cos + part_im * sin
        im = part_im * cos - part_re * sin
        re = re + pltpu.roll(re, 64, 1)
        im = im + pltpu.roll(im, 64, 1)
        re = re + pltpu.roll(re, 32, 1)
        im = im + pltpu.roll(im, 32, 1)
        at = pl.ds(pl.multiple_of(slot * BINS, 8), BINS)
        spec_re[at, :] = re
        spec_im[at, :] = im
        return power + re * re + im * im

    power = lax.fori_loop(0, HALF, bands, jnp.zeros((BINS, 128), f32), unroll=2)
    parity = lax.broadcasted_iota(jnp.int32, (BINS, 128), 0) % 2
    other = jnp.where(parity == 0, pltpu.roll(power, BINS - 1, 0), pltpu.roll(power, 1, 0))
    gain = lax.rsqrt((power + other) / SPLIT + EPSILON)
    gain = jnp.concatenate([gain, gain], 0)

    def whiten(index, carry):
        at = pl.ds(pl.multiple_of(index * 2 * BINS, 16), 2 * BINS)
        re_ref[at, :] = (spec_re[at, :] * gain).astype(bf16)
        im_ref[at, :] = (spec_im[at, :] * gain).astype(bf16)
        return carry

    lax.fori_loop(0, HALF // 2, whiten, 0, unroll=2)
    group = lax.broadcasted_iota(jnp.int32, (64, 128), 1) // 16

    def pack(index, carry):
        for k, ref in enumerate((re_ref, im_ref)):
            parts = []
            for g in range(8):
                at = pl.ds(pl.multiple_of(g * 320 + index * 64, 64), 64)
                part = ref[at, :].astype(f32)
                parts.append(pltpu.roll(part, 16, 1) if g % 2 else part)
            packed = parts[0]
            for g in range(1, 8):
                packed = jnp.where(group == g, parts[g], packed)
            edge_ref[k, pl.ds(pl.multiple_of(index * 64, 64), 64), :] = packed.astype(bf16)
        return carry

    lax.fori_loop(0, 5, pack, 0)


def spectrum(z):
    weights, cos, sin = second_tables()
    vmem = pl.BlockSpec(memory_space=pltpu.VMEM)
    return pl.pallas_call(
        spectrum_kernel,
        name="spectrum",
        out_shape=[
            jax.ShapeDtypeStruct((NBINS, 128), bf16),
            jax.ShapeDtypeStruct((NBINS, 128), bf16),
            jax.ShapeDtypeStruct((2, NBINS // 8, 128), bf16),
        ],
        in_specs=[vmem] * 5,
        out_specs=[vmem] * 3,
        scratch_shapes=[
            pltpu.VMEM((PAIR * 1024, 128), f32),
            pltpu.VMEM((32, 128, 128), f32),
            pltpu.VMEM((NBINS, 128), f32),
            pltpu.VMEM((NBINS, 128), f32),
        ],
        compiler_params=pltpu.CompilerParams(vmem_limit_bytes=VMEM),
    )(z, jnp.asarray(first_table()), jnp.asarray(weights), jnp.asarray(cos), jnp.asarray(sin))


def correlate_kernel(re_ref, im_ref, edge_ref, mask_ref, cos_ref, sin_ref, order_ref, out_ref, wrap_ref, cross_re, cross_im):
    lane = lax.broadcasted_iota(jnp.int32, (64, 128), 1)
    inner = lane < 32
    slot = lane // 32

    def cross(index, carry):
        group, part = index // 5, index % 5
        at = pl.ds(pl.multiple_of(index * 64, 64), 64)
        edge_at = pl.ds(pl.multiple_of(part * 64, 64), 64)
        own, ahead = [], []
        for k, ref in enumerate((re_ref, im_ref)):
            mine = ref[at, :].astype(f32)
            edge = pltpu.roll(edge_ref[k, edge_at, :].astype(f32), lax.rem(160 - 16 * group, 128), 1)
            own.append(mine)
            ahead.append(jnp.where(inner, mine, edge))
        a, f = own
        for tile in range(2):
            other = []
            for whole in ahead:
                shifted = None
                for k in range(4):
                    shift = (32 * k - 2 * (4 * tile + k + 1)) % 128
                    moved = pltpu.roll(whole, shift, 1)
                    shifted = moved if k == 0 else jnp.where(slot == k, moved, shifted)
                other.append(shifted)
            e, g = other
            columns = pl.ds(128 * tile, 128)
            cross_re[at, columns] = (a * e + f * g).astype(bf16)
            cross_im[at, columns] = (f * e - a * g).astype(bf16)
        return carry

    lax.fori_loop(0, 40, cross, 0)
    inv_root = 1.0 / math.sqrt(NBINS)
    present = mask_ref[...] > 0.5
    results = []
    even = jnp.dot(cos_ref[...], cross_re[...], preferred_element_type=f32)
    odd = jnp.dot(sin_ref[...], cross_im[...], preferred_element_type=f32)
    for half in (even - odd, even + odd):
        results.append(jnp.where(present, half * inv_root, 0.0).astype(bf16))
    halves = jnp.concatenate(results, 1)
    got = lax.dot_general(
        order_ref[...], halves, (((1,), (1,)), ((), ())), preferred_element_type=f32
    )
    for block in range(ROW):
        out_ref[block] = got[32 * block : 32 * block + 32].astype(bf16)
    for block in range(REACH):
        both = [got[32 * block + 16 * e + 8 : 32 * block + 16 * e + 16] for e in range(2)]
        wrap_ref[block] = jnp.concatenate(both, 0).astype(bf16)


def correlate(re, im, edge, mask):
    cos, sin = lag_tables()
    vmem = pl.BlockSpec(memory_space=pltpu.VMEM)
    return pl.pallas_call(
        correlate_kernel,
        name="correlate",
        out_shape=[
            jax.ShapeDtypeStruct((ROW, 32, LAG), bf16),
            jax.ShapeDtypeStruct((REACH, 16, LAG), bf16),
        ],
        in_specs=[vmem] * 7,
        out_specs=[vmem] * 2,
        scratch_shapes=[pltpu.VMEM((NBINS, 256), bf16), pltpu.VMEM((NBINS, 256), bf16)],
        compiler_params=pltpu.CompilerParams(vmem_limit_bytes=VMEM),
    )(re, im, edge, mask, jnp.asarray(cos), jnp.asarray(sin), jnp.asarray(order_table()))


def deliver_kernel(part_ref, wrap_ref, out_ref, prev_ref, send_sem, recv_sem, ws_sem, wr_sem, own_sem):
    me, worker = lax.axis_index("blk"), lax.axis_index("pair")
    row, place = me // ROW, me % ROW
    behind = lax.rem(row + NROW - 1, NROW) * ROW
    ahead = lax.rem(row + 1, NROW) * ROW
    barrier = pltpu.get_barrier_semaphore()

    def greet(step, carry):
        there = row * ROW + lax.rem(place + step, ROW)
        pl.semaphore_signal(barrier, inc=1, device_id=(there, worker), device_id_type=MESH)
        return carry

    def greet_behind(step, carry):
        pl.semaphore_signal(barrier, inc=1, device_id=(behind + step, worker), device_id_type=MESH)
        return carry

    lax.fori_loop(1, ROW, greet, 0)

    @pl.when(place < REACH)
    def _():
        lax.fori_loop(0, ROW, greet_behind, 0)

    pl.semaphore_wait(barrier, ROW - 1 + REACH)

    def send(step, carry):
        to = lax.rem(place + step, ROW)
        pltpu.make_async_remote_copy(
            src_ref=part_ref.at[to],
            dst_ref=out_ref.at[place],
            send_sem=send_sem,
            recv_sem=recv_sem,
            device_id=(row * ROW + to, worker),
            device_id_type=MESH,
        ).start()
        return carry

    def send_ahead(step, carry):
        to = lax.rem(place + step, REACH)
        pltpu.make_async_remote_copy(
            src_ref=wrap_ref.at[to],
            dst_ref=prev_ref.at[place],
            send_sem=ws_sem,
            recv_sem=wr_sem,
            device_id=(ahead + to, worker),
            device_id_type=MESH,
        ).start()
        return carry

    lax.fori_loop(0, REACH, send_ahead, 0)
    lax.fori_loop(1, ROW, send, 0)
    own = pltpu.make_async_copy(part_ref.at[place], out_ref.at[place], own_sem)
    own.start()
    own.wait()
    pltpu.make_async_remote_copy(
        src_ref=part_ref.at[pl.ds(0, ROW - 1)],
        dst_ref=out_ref.at[pl.ds(0, ROW - 1)],
        send_sem=send_sem,
        recv_sem=recv_sem,
        device_id=(ahead + place, worker),
        device_id_type=MESH,
    ).wait()
    wrapped = pltpu.make_async_remote_copy(
        src_ref=wrap_ref,
        dst_ref=prev_ref.at[pl.ds(0, REACH)],
        send_sem=ws_sem,
        recv_sem=wr_sem,
        device_id=(ahead + place, worker),
        device_id_type=MESH,
    )
    wrapped.wait_send()

    @pl.when(place < REACH)
    def _():
        pltpu.make_async_remote_copy(
            src_ref=prev_ref,
            dst_ref=prev_ref,
            send_sem=ws_sem,
            recv_sem=wr_sem,
            device_id=(ahead + place, worker),
            device_id_type=MESH,
        ).wait_recv()


def deliver(part, wrap):
    vmem = pl.BlockSpec(memory_space=pltpu.VMEM)
    return pl.pallas_call(
        deliver_kernel,
        name="deliver",
        out_shape=[
            jax.ShapeDtypeStruct((ROW, 32, LAG), bf16),
            jax.ShapeDtypeStruct((ROW, 16, LAG), bf16),
        ],
        in_specs=[vmem] * 2,
        out_specs=[pl.BlockSpec(memory_space=pl.ANY)] * 2,
        scratch_shapes=[pltpu.SemaphoreType.DMA] * 5,
        compiler_params=pltpu.CompilerParams(
            collective_id=1, has_side_effects=True, vmem_limit_bytes=VMEM
        ),
    )(part, wrap)


def shards(raw, pair_list):
    me = lax.axis_index("blk")
    row, place = me // ROW, me % ROW
    z = regroup(raw)
    re, im, edge = spectrum(z)
    ring = [((i + ROW) % SPLIT, i) for i in range(SPLIT)]
    edge = lax.ppermute(edge, "blk", ring)
    column = jnp.arange(256, dtype=jnp.int32)
    leading = row * ROW + (column // 2) % ROW
    wanted = jnp.stack([leading, leading + column // 32 + 1], 0)
    found = (pair_list[:, 0, None] == wanted[0]) & (pair_list[:, 1, None] == wanted[1])
    mask = jnp.max(found.astype(f32), axis=0, keepdims=True)
    part, wrap = correlate(re, im, edge, mask)
    out, prev = deliver(part, wrap)
    out = out.reshape(32, 16, LAG).astype(f32)
    prev = prev.reshape(32, REACH, LAG).astype(f32)
    late = (jnp.arange(REACH) >= place)[None, :, None]
    far = jnp.where(late, prev, out[:, REACH:])
    return jnp.concatenate([out[:, :REACH], far], 1)[None]


def solution(mesh):
    return jax.shard_map(
        shards,
        mesh=mesh,
        in_specs=(P("blk", "pair", None), P()),
        out_specs=P("blk", "pair", None, None),
        check_vma=False,
    )
```

```python
import math

import jax
import jax.numpy as jnp
import ml_dtypes
import numpy as np
from jax import lax
from jax.experimental import pallas as pl
from jax.experimental.pallas import tpu as pltpu
from jax.sharding import PartitionSpec as P

SPLIT = 128
NT = SPLIT * SPLIT
NBAND = 20
REACH = 8
LAG = 512
ROW = 16
NROW = 8
PAIR = 4
HALF = SPLIT // 2
BINS = 2 * NBAND
NBINS = HALF * BINS
EPSILON = 1e-06
VMEM = 56 * 1024 * 1024
MESH = pl.DeviceIdType.MESH
bf16 = jnp.bfloat16
f32 = jnp.float32


def first_table():
    angle = 2.0 * np.pi / SPLIT * (np.outer(np.arange(SPLIT), np.arange(SPLIT)) % SPLIT)
    table = np.concatenate([np.cos(angle[: HALF + 1]), -np.sin(angle[1:HALF])])
    return table.astype(ml_dtypes.bfloat16)


def slot_bins():
    slot = np.arange(HALF)[:, None, None]
    band = np.arange(NBAND)[None, :, None]
    mirror = np.where(slot == 0, HALF, SPLIT - slot)
    low = np.where(np.arange(2)[None, None, :] == 0, slot, mirror)
    return (low + SPLIT * band).reshape(HALF, BINS)


def angle_of(product):
    return 2.0 * np.pi / NT * (product % NT)


def second_tables():
    bins = slot_bins()
    worker, h = np.arange(PAIR)[:, None], np.arange(8)[None, :]
    sample = (32 * worker + h).reshape(-1)
    phi = angle_of(bins[:, :, None] * sample)
    cos, sin = np.cos(phi), np.sin(phi)
    sign = np.where(np.arange(BINS) % 2 == 0, 1.0, -1.0)[None, :, None]
    re = np.concatenate([cos, sign * sin], 2)
    im = np.concatenate([-sin, sign * cos], 2)
    zero = np.zeros_like(cos[0])
    even = (np.arange(BINS) % 2 == 0)[:, None]
    re[0] = np.concatenate([np.where(even, cos[0], zero), np.where(even, zero, cos[0])], 1)
    im[0] = np.concatenate([np.where(even, -sin[0], zero), np.where(even, zero, -sin[0])], 1)
    full = np.concatenate([re, im], 1)
    high = full.astype(ml_dtypes.bfloat16)
    low = (full - high.astype(np.float64)).astype(ml_dtypes.bfloat16)
    weights = np.concatenate([high, high, low], 2)
    quarter = np.repeat(8 * np.arange(4), 32)
    psi = angle_of(bins[:, :, None] * quarter)
    return weights, np.cos(psi).astype(np.float32), np.sin(psi).astype(np.float32)


def lag_tables():
    angle = angle_of(np.arange(LAG)[:, None] * slot_bins().reshape(-1)[None, :])
    return np.cos(angle).astype(ml_dtypes.bfloat16), np.sin(angle).astype(ml_dtypes.bfloat16)


def order_tables():
    near = np.zeros((256, 256), ml_dtypes.bfloat16)
    far = np.zeros((256, 256), ml_dtypes.bfloat16)
    for block in range(ROW):
        for e in range(2):
            for d in range(REACH):
                row = block * 16 + e * 8 + d
                near[row, 32 * d + 2 * block + e] = 1
                far[row, 32 * d + 2 * ((block - d - 1) % ROW) + e] = 1
    return np.stack([near, far])


def ahead_table():
    table = np.zeros((8, 256, 256), ml_dtypes.bfloat16)
    for g in range(8):
        for column in range(256):
            c = column % 32 + 2 * (column // 32 + 1)
            table[g, c if c < 32 else 128 + 16 * g + c - 32, column] = 1
    return table


def swap_bits(tiles, bits):
    lane = lax.broadcasted_iota(jnp.int32, tiles[0].shape, 1)
    tiles = list(tiles)
    for bit, shift in bits:
        low_half = (lane & shift) == 0
        for low in range(len(tiles)):
            if low & bit:
                continue
            a, b = tiles[low], tiles[low | bit]
            tiles[low] = jnp.where(low_half, a, pltpu.roll(b, shift, 1))
            tiles[low | bit] = jnp.where(low_half, pltpu.roll(a, 128 - shift, 1), b)
    return tiles


WAVES = ((3, 5), (0, 4), (2, 6), (1, 7))
CHUNKS = 4
CROWS = NBINS // CHUNKS
EROWS = CROWS // 8
TCH = 2
TW = LAG // TCH


def whole_kernel(
    raw_hbm, pair_ref, t_hbm, w_hbm, c_hbm, s_hbm, lc_hbm, ls_hbm, order_hbm, ahead_hbm, out_ref,
    raw_ref, t_ref, w_ref, c_ref, s_ref, lc_ref, ls_ref, order_ref, ahead_ref,
    sent, landed, quarters, zs, wide, first, spec_re, spec_im, white, edge_out, edge_in,
    cross_re, cross_im, near_out, wrap_out, wrap_in, far_out, near_in, far_in,
    load_sem, a_send, a_recv, x_send, x_recv, e_send, e_recv, n_send, n_recv, f_send, f_recv, w_send, w_recv,
):
    me, worker = lax.axis_index("blk"), lax.axis_index("pair")
    row, place = me // ROW, me % ROW
    behind = lax.rem(row + NROW - 1, NROW) * ROW + place
    ahead = lax.rem(row + 1, NROW) * ROW + place

    loads = [
        pltpu.make_async_copy(source, target, load_sem.at[k])
        for k, (source, target) in enumerate(
            (
                (raw_hbm, raw_ref), (t_hbm, t_ref), (w_hbm, w_ref), (c_hbm, c_ref), (s_hbm, s_ref),
                (ahead_hbm, ahead_ref), (lc_hbm, lc_ref), (ls_hbm, ls_ref), (order_hbm, order_ref),
            )
        )
    ]
    for load in loads:
        load.start()

    def remote(source, target, send, recv, blk, pair):
        return pltpu.make_async_remote_copy(
            src_ref=source, dst_ref=target, send_sem=send, recv_sem=recv, device_id=(blk, pair), device_id_type=MESH
        )

    barrier = pltpu.get_barrier_semaphore()

    def greet(step, carry):
        pl.semaphore_signal(
            barrier, inc=1, device_id=(lax.rem(me + step, SPLIT), worker), device_id_type=MESH
        )
        return carry

    lax.fori_loop(1, SPLIT, greet, 0)
    for step in range(1, PAIR):
        pl.semaphore_signal(
            barrier, inc=1, device_id=(me, lax.rem(worker + step, PAIR)), device_id_type=MESH
        )

    loads[0].wait()

    def spread(index, carry):
        to_row, half = index // 2, index % 2
        rows = pl.ds(pl.multiple_of(half * 16, 16), 16)
        tiles = []
        for block in range(ROW):
            at = pl.multiple_of(to_row * 2048 + block * 128, 128)
            tiles.append(raw_ref[0, rows, pl.ds(at, 128)].astype(f32))
        tiles = swap_bits(tiles, [(1, 2), (2, 4), (4, 8), (8, 16)])
        for block in range(ROW):
            sent[to_row * ROW + block, rows, :] = tiles[block].astype(bf16)
        return carry

    lax.fori_loop(0, 16, spread, 0)

    lane = lax.broadcasted_iota(jnp.int32, (1, 256), 1)
    leading = row * ROW + (lane // 2) % ROW
    trailing = leading + lane // 32 + 1
    listed = pair_ref[...]
    found = (listed[:, 0:1] == leading) & (listed[:, 1:2] == trailing)
    present = jnp.max(jnp.where(found, 1.0, 0.0), axis=0, keepdims=True)

    pl.semaphore_wait(barrier, SPLIT - 1 + PAIR - 1)

    for wave, (one, two) in enumerate(WAVES):

        def send(step, carry, wave=wave, one=one, two=two):
            to_row = lax.rem(row + one + (two - one) * (step % 2), NROW)
            shift = ((step // 2) * 7) % 16
            chip = lax.rem(place // 2 + shift // 2, 8)
            there = to_row * ROW + chip * 2 + lax.rem(place % 2 + shift % 2, 2)
            remote(sent.at[there], landed.at[me], a_send, a_recv.at[wave], there, worker).start()
            return carry

        lax.fori_loop(1 if one == 0 else 0, 32, send, 0)
    landed[me] = sent[me]

    for wave, (one, two) in enumerate(WAVES):
        count = 31 if one == 0 else 32
        remote(
            sent.at[pl.ds(0, count)], landed.at[pl.ds(0, count)], a_send, a_recv.at[wave], ahead, worker
        ).wait_recv()
        for distance in (one, two):
            from_row = lax.rem(row + NROW - distance, NROW)

            def quarter(index, carry, from_row=from_row):
                parts = []
                for k in range(2):
                    block = landed[from_row * ROW + index * 2 + k].astype(f32)
                    tiles = [block[8 * q : 8 * q + 8] for q in range(4)]
                    parts.append(swap_bits(tiles, [(1, 32), (2, 64)]))
                at = pl.ds(pl.multiple_of(from_row * 128 + index * 16, 16), 16)
                for w in range(PAIR):
                    quarters[w, at, :] = jnp.concatenate([parts[0][w], parts[1][w]], 0).astype(bf16)
                return carry

            lax.fori_loop(0, 8, quarter, 0, unroll=4)
            at = pl.ds(pl.multiple_of(from_row * 128, 128), 128)
            for step in range(1, PAIR):
                there = lax.rem(worker + step, PAIR)
                remote(
                    quarters.at[there, at], zs.at[worker, at], x_send, x_recv.at[wave], me, there
                ).start()
            zs[worker, at, :] = quarters[worker, at, :]

    for load in loads[1:]:
        load.wait()
    for wave, (one, two) in enumerate(WAVES):
        part = zs.at[pl.ds(0, PAIR - 1), pl.ds(0, 256)]
        remote(part, part, x_send, x_recv.at[wave], me, lax.rem(worker + 1, PAIR)).wait_recv()
        for distance in (one, two):
            from_row = lax.rem(row + NROW - distance, NROW)
            at = pl.multiple_of(from_row * 128, 128)
            for w in range(PAIR):
                wide[pl.ds(1024 * w + at, 128), :] = zs[w, pl.ds(at, 128), :].astype(f32)
    table = t_ref[...]

    def transform(index, carry):
        at = (index // 4) * 1024 + (index % 4) * 2
        pair = [wide[pl.ds(at + k, 128, stride=8), :].astype(bf16) for k in range(2)]
        got = jnp.dot(table, jnp.concatenate(pair, 1), preferred_element_type=f32)
        first[index * 2] = got[:, :128]
        first[index * 2 + 1] = got[:, 128:]
        return carry

    lax.fori_loop(0, 16, transform, 0, unroll=8)
    flat = first.reshape(32 * 128, 128)

    def bands(slot, power):
        a = flat[pl.ds(slot, 32, stride=128), :]
        b = flat[pl.ds(slot + HALF, 32, stride=128), :]
        both = jnp.concatenate([a, b], 0)
        high = both.astype(bf16)
        low = (both - high.astype(f32)).astype(bf16)
        got = jnp.dot(
            w_ref[slot], jnp.concatenate([high, low, high], 0), preferred_element_type=f32
        )
        part_re, part_im = got[:BINS], got[BINS:]
        cos, sin = c_ref[slot], s_ref[slot]
        re = part_re * cos + part_im * sin
        im = part_im * cos - part_re * sin
        re = re + pltpu.roll(re, 64, 1)
        im = im + pltpu.roll(im, 64, 1)
        re = re + pltpu.roll(re, 32, 1)
        im = im + pltpu.roll(im, 32, 1)
        at = pl.ds(pl.multiple_of(slot * BINS, 8), BINS)
        spec_re[at, :] = re
        spec_im[at, :] = im
        return power + re * re + im * im

    power = lax.fori_loop(0, HALF, bands, jnp.zeros((BINS, 128), f32), unroll=8)
    parity = lax.broadcasted_iota(jnp.int32, (BINS, 128), 0) % 2
    other = jnp.where(parity == 0, pltpu.roll(power, BINS - 1, 0), pltpu.roll(power, 1, 0))
    gain = lax.rsqrt((power + other) / SPLIT + EPSILON)
    gain = jnp.concatenate([gain, gain], 0)
    group = lax.broadcasted_iota(jnp.int32, (EROWS, 128), 1) // 16

    for chunk in range(CHUNKS):
        for k, spec in enumerate((spec_re, spec_im)):
            packed = None
            for g in range(8):
                at = pl.ds(CROWS * chunk + EROWS * g, EROWS)
                value = (spec[at, :] * gain).astype(bf16)
                white[k, at, :] = value
                value = value.astype(f32)
                value = pltpu.roll(value, 16, 1) if g % 2 else value
                packed = value if g == 0 else jnp.where(group == g, value, packed)
            edge_out[chunk, k] = packed.astype(bf16)
        remote(
            edge_out.at[chunk], edge_in.at[chunk], e_send.at[chunk], e_recv.at[chunk], behind, worker
        ).start()

    for chunk in range(CHUNKS):
        remote(
            edge_out.at[chunk], edge_in.at[chunk], e_send.at[chunk], e_recv.at[chunk], behind, worker
        ).wait()

        def cross(g, carry, chunk=chunk):
            at = pl.ds(pl.multiple_of(CROWS * chunk + EROWS * g, 16), EROWS)
            own = [white[k, at, :] for k in range(2)]
            both = [jnp.concatenate([own[k], edge_in[chunk, k]], 1) for k in range(2)]
            got = jnp.dot(
                jnp.concatenate(both, 0), ahead_ref[g], preferred_element_type=f32
            )
            a, f = own[0].astype(f32), own[1].astype(f32)
            for tile in range(2):
                columns = slice(128 * tile, 128 * tile + 128)
                e, h = got[:EROWS, columns], got[EROWS:, columns]
                cross_re[at, columns] = (a * e + f * h).astype(bf16)
                cross_im[at, columns] = (f * e - a * h).astype(bf16)
            return carry

        lax.fori_loop(0, 8, cross, 0, unroll=2)

    inv_root = 1.0 / math.sqrt(NBINS)
    offset = lax.broadcasted_iota(jnp.int32, (16, TW), 0) % REACH
    nt = (((1,), (1,)), ((), ()))
    for t in range(TCH):
        lags = pl.ds(TW * t, TW)
        even = jnp.dot(lc_ref[lags, :], cross_re[...], preferred_element_type=f32)
        odd = jnp.dot(ls_ref[lags, :], cross_im[...], preferred_element_type=f32)
        near, far = (
            jnp.where(present > 0.5, half * inv_root, 0.0).astype(bf16)
            for half in (even - odd, even + odd)
        )
        far = lax.dot_general(order_ref[1], far, nt, preferred_element_type=f32).astype(bf16)
        wrap_out[t] = far[: 16 * REACH]
        far_out[t] = far
        remote(wrap_out.at[t], wrap_in.at[t], w_send.at[t], w_recv.at[t], ahead, worker).start()
        near = lax.dot_general(order_ref[0], near, nt, preferred_element_type=f32).astype(bf16)
        near_out[t] = near.reshape(ROW, 16, TW)

        def send_near(step, carry, t=t):
            to = lax.rem(place + (step * 7) % 16, ROW)
            remote(
                near_out.at[t, to], near_in.at[t, place], n_send, n_recv.at[t], row * ROW + to, worker
            ).start()
            return carry

        lax.fori_loop(1, ROW, send_near, 0)

    for t in range(TCH):
        remote(wrap_out.at[t], wrap_in.at[t], w_send.at[t], w_recv.at[t], ahead, worker).wait()
        for block in range(REACH):
            at = pl.ds(16 * block, 16)
            far_out[t, at, :] = jnp.where(
                offset < block, far_out[t, at, :].astype(f32), wrap_in[t, at, :].astype(f32)
            ).astype(bf16)

        def send_far(step, carry, t=t):
            to = lax.rem(place + (step * 7) % 16, ROW)
            at = pl.ds(pl.multiple_of(to * 16, 16), 16)
            remote(
                far_out.at[t, at], far_in.at[t, place], f_send, f_recv.at[t], row * ROW + to, worker
            ).start()
            return carry

        lax.fori_loop(1, ROW, send_far, 0)

    for t in range(TCH):
        near_in[t, place] = near_out[t, place]
        far_in[t, place] = far_out[t, pl.ds(pl.multiple_of(place * 16, 16), 16), :]
    for half, (arrived, send, recv) in enumerate(((near_in, n_send, n_recv), (far_in, f_send, f_recv))):
        for t in range(TCH):
            most = arrived.at[t, pl.ds(0, ROW - 1)]
            remote(most, most, send, recv.at[t], ahead, worker).wait_recv()

            def store(r, carry, arrived=arrived, t=t, half=half):
                value = arrived[t, r].astype(f32)
                for e in range(2):
                    out_ref[0, 2 * r + e, 8 * half : 8 * half + 8, TW * t : TW * t + TW] = value[8 * e : 8 * e + 8]
                return carry

            lax.fori_loop(0, ROW, store, 0, unroll=4)

    most = sent.at[pl.ds(0, SPLIT - 1)]
    remote(most, most, a_send, a_recv.at[0], ahead, worker).wait_send()
    most = quarters.at[pl.ds(0, PAIR - 1)]
    remote(most, most, x_send, x_recv.at[0], ahead, worker).wait_send()
    most = near_in.at[:, pl.ds(0, ROW - 1)]
    remote(most, most, n_send, n_recv.at[0], ahead, worker).wait_send()
    most = far_in.at[:, pl.ds(0, ROW - 1)]
    remote(most, most, f_send, f_recv.at[0], ahead, worker).wait_send()


def shards(raw, pair_list):
    weights, cos, sin = second_tables()
    lag_cos, lag_sin = lag_tables()
    tables = [first_table(), weights, cos, sin, lag_cos, lag_sin, order_tables(), ahead_table()]
    anywhere = pl.BlockSpec(memory_space=pl.ANY)
    vmem = pl.BlockSpec(memory_space=pltpu.VMEM)
    dma = pltpu.SemaphoreType.DMA
    return pl.pallas_call(
        whole_kernel,
        name="whole",
        out_shape=jax.ShapeDtypeStruct((1, 32, 2 * REACH, LAG), f32),
        in_specs=[anywhere, vmem] + [anywhere] * len(tables),
        out_specs=vmem,
        scratch_shapes=[
            pltpu.VMEM(raw.shape, bf16),
            *(pltpu.VMEM(table.shape, table.dtype) for table in tables),
            pltpu.VMEM((SPLIT, 32, 128), bf16),
            pltpu.VMEM((SPLIT, 32, 128), bf16),
            pltpu.VMEM((PAIR, 1024, 128), bf16),
            pltpu.VMEM((PAIR, 1024, 128), bf16),
            pltpu.VMEM((PAIR * 1024, 128), f32),
            pltpu.VMEM((32, 128, 128), f32),
            pltpu.VMEM((NBINS, 128), f32),
            pltpu.VMEM((NBINS, 128), f32),
            pltpu.VMEM((2, NBINS, 128), bf16),
            pltpu.VMEM((CHUNKS, 2, EROWS, 128), bf16),
            pltpu.VMEM((CHUNKS, 2, EROWS, 128), bf16),
            pltpu.VMEM((NBINS, 256), bf16),
            pltpu.VMEM((NBINS, 256), bf16),
            pltpu.VMEM((TCH, ROW, 16, TW), bf16),
            pltpu.VMEM((TCH, 16 * REACH, TW), bf16),
            pltpu.VMEM((TCH, 16 * REACH, TW), bf16),
            pltpu.VMEM((TCH, 16 * ROW, TW), bf16),
            pltpu.VMEM((TCH, ROW, 16, TW), bf16),
            pltpu.VMEM((TCH, ROW, 16, TW), bf16),
            dma((9,)),
            dma,
            dma((4,)),
            dma,
            dma((4,)),
            dma((CHUNKS,)),
            dma((CHUNKS,)),
            dma,
            dma((TCH,)),
            dma,
            dma((TCH,)),
            dma((TCH,)),
            dma((TCH,)),
        ],
        compiler_params=pltpu.CompilerParams(
            collective_id=0, has_side_effects=True, vmem_limit_bytes=VMEM
        ),
    )(raw, pair_list, *(jnp.asarray(table) for table in tables))


def solution(mesh):
    return jax.shard_map(
        shards,
        mesh=mesh,
        in_specs=(P("blk", "pair", None), P()),
        out_specs=P("blk", "pair", None, None),
        check_vma=False,
    )
```

```python
import math

import jax
import jax.numpy as jnp
import ml_dtypes
import numpy as np
from jax import lax
from jax.experimental import pallas as pl
from jax.experimental.pallas import tpu as pltpu
from jax.sharding import PartitionSpec as P

SPLIT = 128
NT = SPLIT * SPLIT
NBAND = 20
REACH = 8
LAG = 512
ROW = 16
NROW = 8
PAIR = 4
HALF = SPLIT // 2
BINS = 2 * NBAND
NBINS = HALF * BINS
EPSILON = 1e-06
VMEM = 56 * 1024 * 1024
MESH = pl.DeviceIdType.MESH
bf16 = jnp.bfloat16
f32 = jnp.float32


def first_table():
    angle = 2.0 * np.pi / SPLIT * (np.outer(np.arange(SPLIT), np.arange(SPLIT)) % SPLIT)
    table = np.concatenate([np.cos(angle[: HALF + 1]), -np.sin(angle[1:HALF])])
    return table.astype(ml_dtypes.bfloat16)


def slot_bins():
    slot = np.arange(HALF)[:, None, None]
    band = np.arange(NBAND)[None, :, None]
    mirror = np.where(slot == 0, HALF, SPLIT - slot)
    low = np.where(np.arange(2)[None, None, :] == 0, slot, mirror)
    return (low + SPLIT * band).reshape(HALF, BINS)


def angle_of(product):
    return 2.0 * np.pi / NT * (product % NT)


def second_tables():
    bins = slot_bins()
    worker, h = np.arange(PAIR)[:, None], np.arange(8)[None, :]
    sample = (32 * worker + h).reshape(-1)
    phi = angle_of(bins[:, :, None] * sample)
    cos, sin = np.cos(phi), np.sin(phi)
    sign = np.where(np.arange(BINS) % 2 == 0, 1.0, -1.0)[None, :, None]
    re = np.concatenate([cos, sign * sin], 2)
    im = np.concatenate([-sin, sign * cos], 2)
    zero = np.zeros_like(cos[0])
    even = (np.arange(BINS) % 2 == 0)[:, None]
    re[0] = np.concatenate([np.where(even, cos[0], zero), np.where(even, zero, cos[0])], 1)
    im[0] = np.concatenate([np.where(even, -sin[0], zero), np.where(even, zero, -sin[0])], 1)
    full = np.concatenate([re, im], 1)
    high = full.astype(ml_dtypes.bfloat16)
    low = (full - high.astype(np.float64)).astype(ml_dtypes.bfloat16)
    weights = np.concatenate([high, high, low], 2)
    quarter = np.repeat(8 * np.arange(4), 32)
    psi = angle_of(bins[:, :, None] * quarter)
    return weights, np.cos(psi).astype(np.float32), np.sin(psi).astype(np.float32)


def lag_tables():
    angle = angle_of(np.arange(LAG)[:, None] * slot_bins().reshape(-1)[None, :])
    return np.cos(angle).astype(ml_dtypes.bfloat16), np.sin(angle).astype(ml_dtypes.bfloat16)


def order_tables():
    near = np.zeros((256, 256), ml_dtypes.bfloat16)
    far = np.zeros((256, 256), ml_dtypes.bfloat16)
    for block in range(ROW):
        for e in range(2):
            for d in range(REACH):
                row = block * 16 + e * 8 + d
                near[row, 32 * d + 2 * block + e] = 1
                far[row, 32 * d + 2 * ((block - d - 1) % ROW) + e] = 1
    return np.stack([near, far])


def ahead_table():
    table = np.zeros((8, 256, 256), ml_dtypes.bfloat16)
    for g in range(8):
        for column in range(256):
            c = column % 32 + 2 * (column // 32 + 1)
            table[g, c if c < 32 else 128 + 16 * g + c - 32, column] = 1
    return table


def swap_bits(tiles, bits):
    lane = lax.broadcasted_iota(jnp.int32, tiles[0].shape, 1)
    tiles = list(tiles)
    for bit, shift in bits:
        low_half = (lane & shift) == 0
        for low in range(len(tiles)):
            if low & bit:
                continue
            a, b = tiles[low], tiles[low | bit]
            tiles[low] = jnp.where(low_half, a, pltpu.roll(b, shift, 1))
            tiles[low | bit] = jnp.where(low_half, pltpu.roll(a, 128 - shift, 1), b)
    return tiles


WAVES = (1, 7, 4, 2, 6, 3, 5, 0)
LOOK = 3
PITCH = 40
FPITCH = 136
CHUNKS = 4
CROWS = NBINS // CHUNKS
EROWS = CROWS // 8
TCH = 2
TW = LAG // TCH


def whole_kernel(
    raw_hbm, pair_ref, t_hbm, w_hbm, c_hbm, s_hbm, lc_hbm, ls_hbm, order_hbm, ahead_hbm, out_ref,
    raw_ref, t_ref, w_ref, c_ref, s_ref, lc_ref, ls_ref, order_ref, ahead_ref,
    stage, quarters, swapped, sent, landed, wide, first, spec_re, spec_im, white, edge_out, edge_in,
    cross_re, cross_im, present, near_out, wrap_out, wrap_in, far_out, near_in, far_in,
    load_sem, a_send, a_recv, x_send, x_recv, e_send, e_recv, n_send, n_recv, f_send, f_recv, w_send, w_recv,
):
    me, worker = lax.axis_index("blk"), lax.axis_index("pair")
    row, place = me // ROW, me % ROW
    behind = lax.rem(row + NROW - 1, NROW) * ROW + place
    ahead = lax.rem(row + 1, NROW) * ROW + place

    loads = [
        pltpu.make_async_copy(source, target, load_sem.at[k])
        for k, (source, target) in enumerate(
            (
                (raw_hbm, raw_ref), (t_hbm, t_ref), (w_hbm, w_ref), (c_hbm, c_ref), (s_hbm, s_ref),
                (ahead_hbm, ahead_ref), (lc_hbm, lc_ref), (ls_hbm, ls_ref), (order_hbm, order_ref),
            )
        )
    ]
    loads[0].start()

    def remote(source, target, send, recv, blk, pair):
        return pltpu.make_async_remote_copy(
            src_ref=source, dst_ref=target, send_sem=send, recv_sem=recv, device_id=(blk, pair), device_id_type=MESH
        )

    barrier = pltpu.get_barrier_semaphore()

    def greet(step):
        pl.semaphore_signal(
            barrier, inc=1, device_id=(lax.rem(me + step, SPLIT), worker), device_id_type=MESH
        )

    for step in range(1, PAIR):
        pl.semaphore_signal(
            barrier, inc=1, device_id=(me, lax.rem(worker + step, PAIR)), device_id_type=MESH
        )
    lax.fori_loop(113, SPLIT, lambda step, carry: (greet(step), carry)[1], 0)
    loads[0].wait()

    def spread(to_row, greeting):
        for half in range(2):
            for step in range(56 * half + 1, 56 * half + 57):
                if greeting:
                    greet(step)
            rows = pl.ds(16 * half, 16)
            tiles = []
            for block in range(ROW):
                at = pl.multiple_of(to_row * 2048 + block * 128, 128)
                tiles.append(raw_ref[0, rows, pl.ds(at, 128)].astype(f32))
            tiles = swap_bits(tiles, [(1, 2), (2, 4), (4, 8), (8, 16)])
            for block in range(ROW):
                stage[block, rows, :] = tiles[block].astype(bf16)

    def quarter(to_row):
        def some(index, carry):
            parts = []
            for k in range(2):
                block = stage[index * 2 + k].astype(f32)
                tiles = [block[8 * q : 8 * q + 8] for q in range(4)]
                parts.append(swap_bits(tiles, [(1, 32), (2, 64)]))
            at = pl.ds(pl.multiple_of(index * 16, 16), 16)
            for w in range(PAIR):
                quarters[w, to_row, at, :] = jnp.concatenate([parts[0][w], parts[1][w]], 0).astype(bf16)
            return carry

        lax.fori_loop(0, 8, some, 0, unroll=4)

    def prepare(wave):
        to_row = lax.rem(row + WAVES[wave], NROW)
        spread(to_row, wave == 0)
        quarter(to_row)

    def swap_workers(wave):
        to_row = lax.rem(row + WAVES[wave], NROW)
        for step in range(1, PAIR):
            there = lax.rem(worker + step, PAIR)
            remote(
                quarters.at[there, to_row], swapped.at[worker, to_row], x_send, x_recv.at[wave], me, there
            ).start()
        swapped[worker, to_row] = quarters[worker, to_row]

    def issue(wave):
        to_row = lax.rem(row + WAVES[wave], NROW)
        part = swapped.at[pl.ds(0, PAIR - 1), 0]
        remote(part, part, x_send, x_recv.at[wave], me, lax.rem(worker + 1, PAIR)).wait_recv()

        def join(index, carry):
            at = pl.ds(pl.multiple_of(index * 16, 16), 16)
            parts = [swapped[w, to_row, at, :].astype(f32) for w in range(PAIR)]
            for k in range(2):
                whole = jnp.concatenate([part[8 * k : 8 * k + 8] for part in parts], 0)
                sent[to_row * ROW + index * 2 + k] = whole.astype(bf16)
            return carry

        lax.fori_loop(0, 8, join, 0, unroll=4)

        def send(step, carry):
            shift = (step * 7) % 16
            chip = lax.rem(place // 2 + shift // 2, 8)
            core = lax.rem(place % 2 + shift % 2, 2)
            there = to_row * ROW + chip * 2 + core
            remote(sent.at[there], landed.at[me], a_send, a_recv.at[wave], there, worker).start()
            return carry

        lax.fori_loop(1, 16, send, 0)
        if WAVES[wave]:
            there = to_row * ROW + place
            remote(sent.at[there], landed.at[me], a_send, a_recv.at[wave], there, worker).start()
        else:
            landed[me] = sent[me]

    prepare(0)
    pl.semaphore_wait(barrier, SPLIT - 1 + PAIR - 1)
    swap_workers(0)
    for wave in range(1, NROW + LOOK):
        if wave < NROW:
            prepare(wave)
            swap_workers(wave)
        if wave >= LOOK:
            issue(wave - LOOK)
        if wave == LOOK:
            for load in loads[1:]:
                load.start()

    index = lax.broadcasted_iota(jnp.int32, (256, 768), 0)
    block, step = index // 16, index % REACH + 1
    for k, leading in enumerate((row * ROW + block, row * ROW + (block - step + ROW) % ROW)):
        found = (pair_ref[0:1, :] == leading) & (pair_ref[1:2, :] == leading + step)
        listed = jnp.max(jnp.where(found, 1.0, 0.0), axis=1, keepdims=True)
        present[k] = jnp.broadcast_to(listed, (256, 128))

    for load in loads[1:]:
        load.wait()
    for wave, distance in enumerate(WAVES):
        count = 15 if distance == 0 else 16
        remote(
            sent.at[pl.ds(0, count)], landed.at[pl.ds(0, count)], a_send, a_recv.at[wave], ahead, worker
        ).wait_recv()
        from_row = lax.rem(row + NROW - distance, NROW)

        def widen(index, carry, from_row=from_row):
            source = from_row * ROW + index
            wide[pl.ds(pl.multiple_of(source * PITCH, 8), 32), :] = landed[source].astype(f32)
            return carry

        lax.fori_loop(0, ROW, widen, 0, unroll=4)
    table = t_ref[...]

    def transform(index, carry):
        pair = [wide[pl.ds(index * 2 + k, 128, stride=PITCH), :].astype(bf16) for k in range(2)]
        got = jnp.dot(table, jnp.concatenate(pair, 1), preferred_element_type=f32)
        for k in range(2):
            first[index * 2 + k, pl.ds(0, 128)] = got[:, 128 * k : 128 * k + 128]
        return carry

    lax.fori_loop(0, 16, transform, 0, unroll=8)
    flat = first.reshape(32 * FPITCH, 128)

    def bands(slot, power):
        a = flat[pl.ds(slot, 32, stride=FPITCH), :]
        b = flat[pl.ds(slot + HALF, 32, stride=FPITCH), :]
        both = jnp.concatenate([a, b], 0)
        high = both.astype(bf16)
        low = (both - high.astype(f32)).astype(bf16)
        got = jnp.dot(
            w_ref[slot], jnp.concatenate([high, low, high], 0), preferred_element_type=f32
        )
        part_re, part_im = got[:BINS], got[BINS:]
        cos, sin = c_ref[slot], s_ref[slot]
        re = part_re * cos + part_im * sin
        im = part_im * cos - part_re * sin
        re = re + pltpu.roll(re, 64, 1)
        im = im + pltpu.roll(im, 64, 1)
        re = re + pltpu.roll(re, 32, 1)
        im = im + pltpu.roll(im, 32, 1)
        at = pl.ds(pl.multiple_of(slot * BINS, 8), BINS)
        spec_re[at, :] = re
        spec_im[at, :] = im
        return power + re * re + im * im

    power = lax.fori_loop(0, HALF, bands, jnp.zeros((BINS, 128), f32), unroll=16)
    parity = lax.broadcasted_iota(jnp.int32, (BINS, 128), 0) % 2
    other = jnp.where(parity == 0, pltpu.roll(power, BINS - 1, 0), pltpu.roll(power, 1, 0))
    gain = lax.rsqrt((power + other) / SPLIT + EPSILON)
    gain = jnp.concatenate([gain, gain], 0)
    group = lax.broadcasted_iota(jnp.int32, (EROWS, 128), 1) // 16

    for chunk in range(CHUNKS):
        for k, spec in enumerate((spec_re, spec_im)):
            packed = None
            for g in range(8):
                at = pl.ds(CROWS * chunk + EROWS * g, EROWS)
                value = (spec[at, :] * gain).astype(bf16)
                white[k, at, :] = value
                value = value.astype(f32)
                value = pltpu.roll(value, 16, 1) if g % 2 else value
                packed = value if g == 0 else jnp.where(group == g, value, packed)
            edge_out[chunk, k] = packed.astype(bf16)
        remote(
            edge_out.at[chunk], edge_in.at[chunk], e_send.at[chunk], e_recv.at[chunk], behind, worker
        ).start()

    for chunk in range(CHUNKS):
        remote(
            edge_out.at[chunk], edge_in.at[chunk], e_send.at[chunk], e_recv.at[chunk], behind, worker
        ).wait()

        def cross(g, carry, chunk=chunk):
            at = pl.ds(pl.multiple_of(CROWS * chunk + EROWS * g, 16), EROWS)
            own = [white[k, at, :] for k in range(2)]
            both = [jnp.concatenate([own[k], edge_in[chunk, k]], 1) for k in range(2)]
            got = jnp.dot(
                jnp.concatenate(both, 0), ahead_ref[g], preferred_element_type=f32
            )
            a, f = own[0].astype(f32), own[1].astype(f32)
            for tile in range(2):
                columns = slice(128 * tile, 128 * tile + 128)
                e, h = got[:EROWS, columns], got[EROWS:, columns]
                cross_re[at, columns] = (a * e + f * h).astype(bf16)
                cross_im[at, columns] = (f * e - a * h).astype(bf16)
            return carry

        lax.fori_loop(0, 8, cross, 0, unroll=2)

    inv_root = 1.0 / math.sqrt(NBINS)
    offset = lax.broadcasted_iota(jnp.int32, (16, TW), 0) % REACH
    nt = (((1,), (1,)), ((), ()))
    for t in range(TCH):
        lags = pl.ds(TW * t, TW)
        even = jnp.dot(lc_ref[lags, :], cross_re[...], preferred_element_type=f32)
        odd = jnp.dot(ls_ref[lags, :], cross_im[...], preferred_element_type=f32)
        near, far = ((half * inv_root).astype(bf16) for half in (even - odd, even + odd))
        near, far = (
            lax.dot_general(order_ref[k], half, nt, preferred_element_type=f32)
            for k, half in enumerate((near, far))
        )
        near, far = (
            jnp.where(jnp.concatenate([present[k]] * (TW // 128), 1) > 0.5, half, 0.0).astype(bf16)
            for k, half in enumerate((near, far))
        )
        wrap_out[t] = far[: 16 * REACH]
        far_out[t] = far
        remote(wrap_out.at[t], wrap_in.at[t], w_send.at[t], w_recv.at[t], ahead, worker).start()
        near_out[t] = near.reshape(ROW, 16, TW)

        def send_near(step, carry, t=t):
            to = lax.rem(place + (step * 7) % 16, ROW)
            remote(
                near_out.at[t, to], near_in.at[t, place], n_send, n_recv.at[t], row * ROW + to, worker
            ).start()
            return carry

        lax.fori_loop(1, ROW, send_near, 0)

    for t in range(TCH):
        remote(wrap_out.at[t], wrap_in.at[t], w_send.at[t], w_recv.at[t], ahead, worker).wait()
        for block in range(REACH):
            at = pl.ds(16 * block, 16)
            far_out[t, at, :] = jnp.where(
                offset < block, far_out[t, at, :].astype(f32), wrap_in[t, at, :].astype(f32)
            ).astype(bf16)

        def send_far(step, carry, t=t):
            to = lax.rem(place + (step * 7) % 16, ROW)
            at = pl.ds(pl.multiple_of(to * 16, 16), 16)
            remote(
                far_out.at[t, at], far_in.at[t, place], f_send, f_recv.at[t], row * ROW + to, worker
            ).start()
            return carry

        lax.fori_loop(1, ROW, send_far, 0)

    for t in range(TCH):
        near_in[t, place] = near_out[t, place]
        far_in[t, place] = far_out[t, pl.ds(pl.multiple_of(place * 16, 16), 16), :]
    for t in range(TCH):
        for arrived, send, recv in ((near_in, n_send, n_recv), (far_in, f_send, f_recv)):
            most = arrived.at[t, pl.ds(0, ROW - 1)]
            remote(most, most, send, recv.at[t], ahead, worker).wait_recv()

        def store(r, carry, t=t):
            near, far = near_in[t, r].astype(f32), far_in[t, r].astype(f32)
            for e in range(2):
                both = jnp.concatenate([near[8 * e : 8 * e + 8], far[8 * e : 8 * e + 8]], 0)
                out_ref[2 * r + e, :, TW * t : TW * t + TW] = both.astype(bf16)
            return carry

        lax.fori_loop(0, ROW, store, 0, unroll=4)

    most = sent.at[pl.ds(0, SPLIT - 1)]
    remote(most, most, a_send, a_recv.at[0], ahead, worker).wait_send()
    most = quarters.at[pl.ds(0, PAIR - 1)]
    remote(most, most, x_send, x_recv.at[0], ahead, worker).wait_send()
    most = near_in.at[:, pl.ds(0, ROW - 1)]
    remote(most, most, n_send, n_recv.at[0], ahead, worker).wait_send()
    most = far_in.at[:, pl.ds(0, ROW - 1)]
    remote(most, most, f_send, f_recv.at[0], ahead, worker).wait_send()


def shards(raw, pair_list):
    weights, cos, sin = second_tables()
    lag_cos, lag_sin = lag_tables()
    tables = [first_table(), weights, cos, sin, lag_cos, lag_sin, order_tables(), ahead_table()]
    anywhere = pl.BlockSpec(memory_space=pl.ANY)
    vmem = pl.BlockSpec(memory_space=pltpu.VMEM)
    dma = pltpu.SemaphoreType.DMA
    halves = pl.pallas_call(
        whole_kernel,
        name="whole",
        out_shape=jax.ShapeDtypeStruct((32, 2 * REACH, LAG), bf16),
        in_specs=[anywhere, vmem] + [anywhere] * len(tables),
        out_specs=vmem,
        scratch_shapes=[
            pltpu.VMEM(raw.shape, bf16),
            *(pltpu.VMEM(table.shape, table.dtype) for table in tables),
            pltpu.VMEM((ROW, 32, 128), bf16),
            pltpu.VMEM((PAIR, NROW, 128, 128), bf16),
            pltpu.VMEM((PAIR, NROW, 128, 128), bf16),
            pltpu.VMEM((SPLIT, 32, 128), bf16),
            pltpu.VMEM((SPLIT, 32, 128), bf16),
            pltpu.VMEM((SPLIT * PITCH, 128), f32),
            pltpu.VMEM((32, FPITCH, 128), f32),
            pltpu.VMEM((NBINS, 128), f32),
            pltpu.VMEM((NBINS, 128), f32),
            pltpu.VMEM((2, NBINS, 128), bf16),
            pltpu.VMEM((CHUNKS, 2, EROWS, 128), bf16),
            pltpu.VMEM((CHUNKS, 2, EROWS, 128), bf16),
            pltpu.VMEM((NBINS, 256), bf16),
            pltpu.VMEM((NBINS, 256), bf16),
            pltpu.VMEM((2, 256, 128), f32),
            pltpu.VMEM((TCH, ROW, 16, TW), bf16),
            pltpu.VMEM((TCH, 16 * REACH, TW), bf16),
            pltpu.VMEM((TCH, 16 * REACH, TW), bf16),
            pltpu.VMEM((TCH, 16 * ROW, TW), bf16),
            pltpu.VMEM((TCH, ROW, 16, TW), bf16),
            pltpu.VMEM((TCH, ROW, 16, TW), bf16),
            dma((9,)),
            dma,
            dma((len(WAVES),)),
            dma,
            dma((len(WAVES),)),
            dma((CHUNKS,)),
            dma((CHUNKS,)),
            dma,
            dma((TCH,)),
            dma,
            dma((TCH,)),
            dma((TCH,)),
            dma((TCH,)),
        ],
        compiler_params=pltpu.CompilerParams(
            collective_id=0, has_side_effects=True, vmem_limit_bytes=VMEM
        ),
    )(raw, pair_list.T, *(jnp.asarray(table) for table in tables))
    return halves.astype(f32)[None]


def solution(mesh):
    return jax.shard_map(
        shards,
        mesh=mesh,
        in_specs=(P("blk", "pair", None), P()),
        out_specs=P("blk", "pair", None, None),
        check_vma=False,
    )
```

```python
import math

import jax
import jax.numpy as jnp
import ml_dtypes
import numpy as np
from jax import lax
from jax.experimental import pallas as pl
from jax.experimental.pallas import tpu as pltpu
from jax.sharding import PartitionSpec as P

SPLIT = 128
NT = SPLIT * SPLIT
NBAND = 20
REACH = 8
LAG = 512
ROW = 16
NROW = 8
PAIR = 4
HALF = SPLIT // 2
BINS = 2 * NBAND
NBINS = HALF * BINS
EPSILON = 1e-06
VMEM = 56 * 1024 * 1024
MESH = pl.DeviceIdType.MESH
bf16 = jnp.bfloat16
f32 = jnp.float32


def first_table():
    angle = 2.0 * np.pi / SPLIT * (np.outer(np.arange(SPLIT), np.arange(SPLIT)) % SPLIT)
    table = np.concatenate([np.cos(angle[: HALF + 1]), -np.sin(angle[1:HALF])])
    return table.astype(ml_dtypes.bfloat16)


def slot_bins():
    slot = np.arange(HALF)[:, None, None]
    band = np.arange(NBAND)[None, :, None]
    mirror = np.where(slot == 0, HALF, SPLIT - slot)
    low = np.where(np.arange(2)[None, None, :] == 0, slot, mirror)
    return (low + SPLIT * band).reshape(HALF, BINS)


def angle_of(product):
    return 2.0 * np.pi / NT * (product % NT)


def second_tables():
    bins = slot_bins()
    worker, h = np.arange(PAIR)[:, None], np.arange(8)[None, :]
    sample = (32 * worker + h).reshape(-1)
    phi = angle_of(bins[:, :, None] * sample)
    cos, sin = np.cos(phi), np.sin(phi)
    sign = np.where(np.arange(BINS) % 2 == 0, 1.0, -1.0)[None, :, None]
    re = np.concatenate([cos, sign * sin], 2)
    im = np.concatenate([-sin, sign * cos], 2)
    zero = np.zeros_like(cos[0])
    even = (np.arange(BINS) % 2 == 0)[:, None]
    re[0] = np.concatenate([np.where(even, cos[0], zero), np.where(even, zero, cos[0])], 1)
    im[0] = np.concatenate([np.where(even, -sin[0], zero), np.where(even, zero, -sin[0])], 1)
    full = np.concatenate([re, im], 1)
    high = full.astype(ml_dtypes.bfloat16)
    low = (full - high.astype(np.float64)).astype(ml_dtypes.bfloat16)
    weights = np.concatenate([high, high, low], 2)
    quarter = np.repeat(8 * np.arange(4), 32)
    psi = angle_of(bins[:, :, None] * quarter)
    return weights, np.cos(psi).astype(np.float32), np.sin(psi).astype(np.float32)


def lag_tables():
    angle = angle_of(np.arange(LAG)[:, None] * slot_bins().reshape(-1)[None, :])
    return np.cos(angle).astype(ml_dtypes.bfloat16), np.sin(angle).astype(ml_dtypes.bfloat16)


def order_tables():
    near = np.zeros((256, 256), ml_dtypes.bfloat16)
    far = np.zeros((256, 256), ml_dtypes.bfloat16)
    for block in range(ROW):
        for e in range(2):
            for d in range(REACH):
                row = block * 16 + e * 8 + d
                near[row, 32 * d + 2 * block + e] = 1
                far[row, 32 * d + 2 * ((block - d - 1) % ROW) + e] = 1
    return np.stack([near, far])


def ahead_table():
    table = np.zeros((8, 256, 256), ml_dtypes.bfloat16)
    for g in range(8):
        for column in range(256):
            c = column % 32 + 2 * (column // 32 + 1)
            table[g, c if c < 32 else 128 + 16 * g + c - 32, column] = 1
    return table


def swap_bits(tiles, bits):
    lane = lax.broadcasted_iota(jnp.int32, tiles[0].shape, 1)
    tiles = list(tiles)
    for bit, shift in bits:
        low_half = (lane & shift) == 0
        for low in range(len(tiles)):
            if low & bit:
                continue
            a, b = tiles[low], tiles[low | bit]
            tiles[low] = jnp.where(low_half, a, pltpu.roll(b, shift, 1))
            tiles[low | bit] = jnp.where(low_half, pltpu.roll(a, 128 - shift, 1), b)
    return tiles


WAVES = (1, 7, 4, 2, 6, 3, 5, 0)
LOOK = 3
PITCH = 40
FPITCH = 136
CHUNKS = 4
CROWS = NBINS // CHUNKS
EROWS = CROWS // 8
TCH = 2
TW = LAG // TCH


def whole_kernel(
    raw_hbm, pair_ref, t_hbm, w_hbm, c_hbm, s_hbm, lc_hbm, ls_hbm, order_hbm, ahead_hbm, out_ref,
    raw_ref, t_ref, w_ref, c_ref, s_ref, lc_ref, ls_ref, order_ref, ahead_ref,
    stage, quarters, swapped, sent, landed, wide, first, spec_re, spec_im, white, edge_out, edge_in,
    cross_re, cross_im, present, near_out, wrap_out, wrap_in, far_out, near_in, far_in,
    load_sem, a_send, a_recv, x_send, x_recv, e_send, e_recv, n_send, n_recv, f_send, f_recv, w_send, w_recv,
):
    me, worker = lax.axis_index("blk"), lax.axis_index("pair")
    row, place = me // ROW, me % ROW
    behind = lax.rem(row + NROW - 1, NROW) * ROW + place
    ahead = lax.rem(row + 1, NROW) * ROW + place

    loads = [
        pltpu.make_async_copy(source, target, load_sem.at[k])
        for k, (source, target) in enumerate(
            (
                (raw_hbm, raw_ref), (t_hbm, t_ref), (w_hbm, w_ref), (c_hbm, c_ref), (s_hbm, s_ref),
                (ahead_hbm, ahead_ref), (lc_hbm, lc_ref), (ls_hbm, ls_ref), (order_hbm, order_ref),
            )
        )
    ]
    loads[0].start()

    def remote(source, target, send, recv, blk, pair):
        return pltpu.make_async_remote_copy(
            src_ref=source, dst_ref=target, send_sem=send, recv_sem=recv, device_id=(blk, pair), device_id_type=MESH
        )

    barrier = pltpu.get_barrier_semaphore()

    def greet(step, carry):
        pl.semaphore_signal(
            barrier, inc=1, device_id=(lax.rem(me + step, SPLIT), worker), device_id_type=MESH
        )
        return carry

    for step in range(1, PAIR):
        pl.semaphore_signal(
            barrier, inc=1, device_id=(me, lax.rem(worker + step, PAIR)), device_id_type=MESH
        )
    lax.fori_loop(1, SPLIT, greet, 0)
    loads[0].wait()

    def spread(to_row):
        for half in range(2):
            rows = pl.ds(16 * half, 16)
            tiles = []
            for block in range(ROW):
                at = pl.multiple_of(to_row * 2048 + block * 128, 128)
                tiles.append(raw_ref[0, rows, pl.ds(at, 128)].astype(f32))
            tiles = swap_bits(tiles, [(1, 2), (2, 4), (4, 8), (8, 16)])
            for block in range(ROW):
                stage[block, rows, :] = tiles[block].astype(bf16)

    def quarter(to_row):
        def some(index, carry):
            parts = []
            for k in range(2):
                block = stage[index * 2 + k].astype(f32)
                tiles = [block[8 * q : 8 * q + 8] for q in range(4)]
                parts.append(swap_bits(tiles, [(1, 32), (2, 64)]))
            at = pl.ds(pl.multiple_of(index * 16, 16), 16)
            for w in range(PAIR):
                quarters[w, to_row, at, :] = jnp.concatenate([parts[0][w], parts[1][w]], 0).astype(bf16)
            return carry

        lax.fori_loop(0, 8, some, 0, unroll=4)

    def prepare(wave):
        to_row = lax.rem(row + WAVES[wave], NROW)
        spread(to_row)
        quarter(to_row)

    def swap_workers(wave):
        to_row = lax.rem(row + WAVES[wave], NROW)
        for step in range(1, PAIR):
            there = lax.rem(worker + step, PAIR)
            remote(
                quarters.at[there, to_row], swapped.at[worker, to_row], x_send, x_recv.at[wave], me, there
            ).start()
        swapped[worker, to_row] = quarters[worker, to_row]

    def issue(wave):
        to_row = lax.rem(row + WAVES[wave], NROW)
        part = swapped.at[pl.ds(0, PAIR - 1), 0]
        remote(part, part, x_send, x_recv.at[wave], me, lax.rem(worker + 1, PAIR)).wait_recv()

        def join(index, carry):
            at = pl.ds(pl.multiple_of(index * 16, 16), 16)
            parts = [swapped[w, to_row, at, :].astype(f32) for w in range(PAIR)]
            for k in range(2):
                whole = jnp.concatenate([part[8 * k : 8 * k + 8] for part in parts], 0)
                sent[to_row * ROW + index * 2 + k] = whole.astype(bf16)
            return carry

        lax.fori_loop(0, 8, join, 0, unroll=4)

        def send(step, carry):
            shift = (step * 9) % 16
            chip = lax.rem(place // 2 + shift // 2, 8)
            core = lax.rem(place % 2 + shift % 2, 2)
            there = to_row * ROW + chip * 2 + core
            remote(sent.at[there], landed.at[me], a_send, a_recv.at[wave], there, worker).start()
            return carry

        lax.fori_loop(1, 16, send, 0)
        if WAVES[wave]:
            there = to_row * ROW + place
            remote(sent.at[there], landed.at[me], a_send, a_recv.at[wave], there, worker).start()
        else:
            landed[me] = sent[me]

    prepare(0)
    pl.semaphore_wait(barrier, SPLIT - 1 + PAIR - 1)
    swap_workers(0)
    for wave in range(1, NROW + LOOK):
        if wave < NROW:
            prepare(wave)
            swap_workers(wave)
        if wave >= LOOK:
            issue(wave - LOOK)
        if wave == LOOK:
            for load in loads[1:]:
                load.start()

    index = lax.broadcasted_iota(jnp.int32, (256, 768), 0)
    block, step = index // 16, index % REACH + 1
    for k, leading in enumerate((row * ROW + block, row * ROW + (block - step + ROW) % ROW)):
        found = (pair_ref[0:1, :] == leading) & (pair_ref[1:2, :] == leading + step)
        listed = jnp.max(jnp.where(found, 1.0, 0.0), axis=1, keepdims=True)
        present[k] = jnp.broadcast_to(listed, (256, 128))

    for load in loads[1:]:
        load.wait()
    for wave, distance in enumerate(WAVES):
        count = 15 if distance == 0 else 16
        remote(
            sent.at[pl.ds(0, count)], landed.at[pl.ds(0, count)], a_send, a_recv.at[wave], ahead, worker
        ).wait_recv()
        from_row = lax.rem(row + NROW - distance, NROW)

        def widen(index, carry, from_row=from_row):
            source = from_row * ROW + index
            wide[pl.ds(pl.multiple_of(source * PITCH, 8), 32), :] = landed[source].astype(f32)
            return carry

        lax.fori_loop(0, ROW, widen, 0, unroll=4)
    table = t_ref[...]

    def transform(index, carry):
        pair = [wide[pl.ds(index * 2 + k, 128, stride=PITCH), :].astype(bf16) for k in range(2)]
        got = jnp.dot(table, jnp.concatenate(pair, 1), preferred_element_type=f32)
        for k in range(2):
            first[index * 2 + k, pl.ds(0, 128)] = got[:, 128 * k : 128 * k + 128]
        return carry

    lax.fori_loop(0, 16, transform, 0, unroll=8)
    flat = first.reshape(32 * FPITCH, 128)

    def bands(slot, power):
        a = flat[pl.ds(slot, 32, stride=FPITCH), :]
        b = flat[pl.ds(slot + HALF, 32, stride=FPITCH), :]
        both = jnp.concatenate([a, b], 0)
        high = both.astype(bf16)
        low = (both - high.astype(f32)).astype(bf16)
        got = jnp.dot(
            w_ref[slot], jnp.concatenate([high, low, high], 0), preferred_element_type=f32
        )
        part_re, part_im = got[:BINS], got[BINS:]
        cos, sin = c_ref[slot], s_ref[slot]
        re = part_re * cos + part_im * sin
        im = part_im * cos - part_re * sin
        re = re + pltpu.roll(re, 64, 1)
        im = im + pltpu.roll(im, 64, 1)
        re = re + pltpu.roll(re, 32, 1)
        im = im + pltpu.roll(im, 32, 1)
        at = pl.ds(pl.multiple_of(slot * BINS, 8), BINS)
        spec_re[at, :] = re
        spec_im[at, :] = im
        return power + re * re + im * im

    power = lax.fori_loop(0, HALF, bands, jnp.zeros((BINS, 128), f32), unroll=16)
    parity = lax.broadcasted_iota(jnp.int32, (BINS, 128), 0) % 2
    other = jnp.where(parity == 0, pltpu.roll(power, BINS - 1, 0), pltpu.roll(power, 1, 0))
    gain = lax.rsqrt((power + other) / SPLIT + EPSILON)
    gain = jnp.concatenate([gain, gain], 0)
    group = lax.broadcasted_iota(jnp.int32, (EROWS, 128), 1) // 16

    for chunk in range(CHUNKS):
        for k, spec in enumerate((spec_re, spec_im)):
            packed = None
            for g in range(8):
                at = pl.ds(CROWS * chunk + EROWS * g, EROWS)
                value = (spec[at, :] * gain).astype(bf16)
                white[k, at, :] = value
                value = value.astype(f32)
                value = pltpu.roll(value, 16, 1) if g % 2 else value
                packed = value if g == 0 else jnp.where(group == g, value, packed)
            edge_out[chunk, k] = packed.astype(bf16)
        remote(
            edge_out.at[chunk], edge_in.at[chunk], e_send.at[chunk], e_recv.at[chunk], behind, worker
        ).start()

    for chunk in range(CHUNKS):
        remote(
            edge_out.at[chunk], edge_in.at[chunk], e_send.at[chunk], e_recv.at[chunk], behind, worker
        ).wait()

        def cross(g, carry, chunk=chunk):
            at = pl.ds(pl.multiple_of(CROWS * chunk + EROWS * g, 16), EROWS)
            own = [white[k, at, :] for k in range(2)]
            both = [jnp.concatenate([own[k], edge_in[chunk, k]], 1) for k in range(2)]
            got = jnp.dot(
                jnp.concatenate(both, 0), ahead_ref[g], preferred_element_type=f32
            )
            a, f = own[0].astype(f32), own[1].astype(f32)
            for tile in range(2):
                columns = slice(128 * tile, 128 * tile + 128)
                e, h = got[:EROWS, columns], got[EROWS:, columns]
                cross_re[at, columns] = (a * e + f * h).astype(bf16)
                cross_im[at, columns] = (f * e - a * h).astype(bf16)
            return carry

        lax.fori_loop(0, 8, cross, 0, unroll=2)

    inv_root = 1.0 / math.sqrt(NBINS)
    offset = lax.broadcasted_iota(jnp.int32, (16, TW), 0) % REACH
    nt = (((1,), (1,)), ((), ()))
    for t in range(TCH):
        lags = pl.ds(TW * t, TW)
        even = jnp.dot(lc_ref[lags, :], cross_re[...], preferred_element_type=f32)
        odd = jnp.dot(ls_ref[lags, :], cross_im[...], preferred_element_type=f32)
        near, far = ((half * inv_root).astype(bf16) for half in (even - odd, even + odd))
        near, far = (
            lax.dot_general(order_ref[k], half, nt, preferred_element_type=f32)
            for k, half in enumerate((near, far))
        )
        near, far = (
            jnp.where(jnp.concatenate([present[k]] * (TW // 128), 1) > 0.5, half, 0.0).astype(bf16)
            for k, half in enumerate((near, far))
        )
        wrap_out[t] = far[: 16 * REACH]
        far_out[t] = far
        remote(wrap_out.at[t], wrap_in.at[t], w_send.at[t], w_recv.at[t], ahead, worker).start()
        near_out[t] = near.reshape(ROW, 16, TW)

        def send_near(step, carry, t=t):
            to = lax.rem(place + (step * 7) % 16, ROW)
            remote(
                near_out.at[t, to], near_in.at[t, place], n_send, n_recv.at[t], row * ROW + to, worker
            ).start()
            return carry

        lax.fori_loop(1, ROW, send_near, 0)

    for t in range(TCH):
        remote(wrap_out.at[t], wrap_in.at[t], w_send.at[t], w_recv.at[t], ahead, worker).wait()
        for block in range(REACH):
            at = pl.ds(16 * block, 16)
            far_out[t, at, :] = jnp.where(
                offset < block, far_out[t, at, :].astype(f32), wrap_in[t, at, :].astype(f32)
            ).astype(bf16)

        def send_far(step, carry, t=t):
            to = lax.rem(place + (step * 7) % 16, ROW)
            at = pl.ds(pl.multiple_of(to * 16, 16), 16)
            remote(
                far_out.at[t, at], far_in.at[t, place], f_send, f_recv.at[t], row * ROW + to, worker
            ).start()
            return carry

        lax.fori_loop(1, ROW, send_far, 0)

    for t in range(TCH):
        near_in[t, place] = near_out[t, place]
        far_in[t, place] = far_out[t, pl.ds(pl.multiple_of(place * 16, 16), 16), :]
    for t in range(TCH):
        for arrived, send, recv in ((near_in, n_send, n_recv), (far_in, f_send, f_recv)):
            most = arrived.at[t, pl.ds(0, ROW - 1)]
            remote(most, most, send, recv.at[t], ahead, worker).wait_recv()

        def store(r, carry, t=t):
            near, far = near_in[t, r].astype(f32), far_in[t, r].astype(f32)
            for e in range(2):
                both = jnp.concatenate([near[8 * e : 8 * e + 8], far[8 * e : 8 * e + 8]], 0)
                out_ref[2 * r + e, :, TW * t : TW * t + TW] = both.astype(bf16)
            return carry

        lax.fori_loop(0, ROW, store, 0, unroll=4)

    most = sent.at[pl.ds(0, SPLIT - 1)]
    remote(most, most, a_send, a_recv.at[0], ahead, worker).wait_send()
    most = quarters.at[pl.ds(0, PAIR - 1)]
    remote(most, most, x_send, x_recv.at[0], ahead, worker).wait_send()
    most = near_in.at[:, pl.ds(0, ROW - 1)]
    remote(most, most, n_send, n_recv.at[0], ahead, worker).wait_send()
    most = far_in.at[:, pl.ds(0, ROW - 1)]
    remote(most, most, f_send, f_recv.at[0], ahead, worker).wait_send()


def shards(raw, pair_list):
    weights, cos, sin = second_tables()
    lag_cos, lag_sin = lag_tables()
    tables = [first_table(), weights, cos, sin, lag_cos, lag_sin, order_tables(), ahead_table()]
    anywhere = pl.BlockSpec(memory_space=pl.ANY)
    vmem = pl.BlockSpec(memory_space=pltpu.VMEM)
    dma = pltpu.SemaphoreType.DMA
    halves = pl.pallas_call(
        whole_kernel,
        name="whole",
        out_shape=jax.ShapeDtypeStruct((32, 2 * REACH, LAG), bf16),
        in_specs=[anywhere, vmem] + [anywhere] * len(tables),
        out_specs=vmem,
        scratch_shapes=[
            pltpu.VMEM(raw.shape, bf16),
            *(pltpu.VMEM(table.shape, table.dtype) for table in tables),
            pltpu.VMEM((ROW, 32, 128), bf16),
            pltpu.VMEM((PAIR, NROW, 128, 128), bf16),
            pltpu.VMEM((PAIR, NROW, 128, 128), bf16),
            pltpu.VMEM((SPLIT, 32, 128), bf16),
            pltpu.VMEM((SPLIT, 32, 128), bf16),
            pltpu.VMEM((SPLIT * PITCH, 128), f32),
            pltpu.VMEM((32, FPITCH, 128), f32),
            pltpu.VMEM((NBINS, 128), f32),
            pltpu.VMEM((NBINS, 128), f32),
            pltpu.VMEM((2, NBINS, 128), bf16),
            pltpu.VMEM((CHUNKS, 2, EROWS, 128), bf16),
            pltpu.VMEM((CHUNKS, 2, EROWS, 128), bf16),
            pltpu.VMEM((NBINS, 256), bf16),
            pltpu.VMEM((NBINS, 256), bf16),
            pltpu.VMEM((2, 256, 128), f32),
            pltpu.VMEM((TCH, ROW, 16, TW), bf16),
            pltpu.VMEM((TCH, 16 * REACH, TW), bf16),
            pltpu.VMEM((TCH, 16 * REACH, TW), bf16),
            pltpu.VMEM((TCH, 16 * ROW, TW), bf16),
            pltpu.VMEM((TCH, ROW, 16, TW), bf16),
            pltpu.VMEM((TCH, ROW, 16, TW), bf16),
            dma((9,)),
            dma,
            dma((len(WAVES),)),
            dma,
            dma((len(WAVES),)),
            dma((CHUNKS,)),
            dma((CHUNKS,)),
            dma,
            dma((TCH,)),
            dma,
            dma((TCH,)),
            dma((TCH,)),
            dma((TCH,)),
        ],
        compiler_params=pltpu.CompilerParams(
            collective_id=0, has_side_effects=True, vmem_limit_bytes=VMEM
        ),
    )(raw, pair_list.T, *(jnp.asarray(table) for table in tables))
    return halves.astype(f32)[None]


def solution(mesh):
    return jax.shard_map(
        shards,
        mesh=mesh,
        in_specs=(P("blk", "pair", None), P()),
        out_specs=P("blk", "pair", None, None),
        check_vma=False,
    )
```

```python
import math

import jax
import jax.numpy as jnp
import ml_dtypes
import numpy as np
from jax import lax
from jax.experimental import pallas as pl
from jax.experimental.pallas import tpu as pltpu
from jax.sharding import PartitionSpec as P

SPLIT = 128
NT = SPLIT * SPLIT
NBAND = 20
REACH = 8
LAG = 512
ROW = 16
NROW = 8
PAIR = 4
HALF = SPLIT // 2
BINS = 2 * NBAND
NBINS = HALF * BINS
EPSILON = 1e-06
VMEM = 56 * 1024 * 1024
MESH = pl.DeviceIdType.MESH
bf16 = jnp.bfloat16
f32 = jnp.float32


def first_table():
    angle = 2.0 * np.pi / SPLIT * (np.outer(np.arange(SPLIT), np.arange(SPLIT)) % SPLIT)
    table = np.concatenate([np.cos(angle[: HALF + 1]), -np.sin(angle[1:HALF])])
    return table.astype(ml_dtypes.bfloat16)


def slot_bins():
    slot = np.arange(HALF)[:, None, None]
    band = np.arange(NBAND)[None, :, None]
    mirror = np.where(slot == 0, HALF, SPLIT - slot)
    low = np.where(np.arange(2)[None, None, :] == 0, slot, mirror)
    return (low + SPLIT * band).reshape(HALF, BINS)


def angle_of(product):
    return 2.0 * np.pi / NT * (product % NT)


def second_tables():
    bins = slot_bins()
    worker, h = np.arange(PAIR)[:, None], np.arange(8)[None, :]
    sample = (32 * worker + h).reshape(-1)
    phi = angle_of(bins[:, :, None] * sample)
    cos, sin = np.cos(phi), np.sin(phi)
    sign = np.where(np.arange(BINS) % 2 == 0, 1.0, -1.0)[None, :, None]
    re = np.concatenate([cos, sign * sin], 2)
    im = np.concatenate([-sin, sign * cos], 2)
    zero = np.zeros_like(cos[0])
    even = (np.arange(BINS) % 2 == 0)[:, None]
    re[0] = np.concatenate([np.where(even, cos[0], zero), np.where(even, zero, cos[0])], 1)
    im[0] = np.concatenate([np.where(even, -sin[0], zero), np.where(even, zero, -sin[0])], 1)
    full = np.concatenate([re, im], 1)
    high = full.astype(ml_dtypes.bfloat16)
    low = (full - high.astype(np.float64)).astype(ml_dtypes.bfloat16)
    weights = np.concatenate([high, high, low], 2)
    quarter = np.repeat(8 * np.arange(4), 32)
    psi = angle_of(bins[:, :, None] * quarter)
    return weights, np.cos(psi).astype(np.float32), np.sin(psi).astype(np.float32)


def lag_tables():
    angle = angle_of(np.arange(LAG)[:, None] * slot_bins().reshape(-1)[None, :])
    return np.cos(angle).astype(ml_dtypes.bfloat16), np.sin(angle).astype(ml_dtypes.bfloat16)


def order_tables():
    near = np.zeros((256, 256), ml_dtypes.bfloat16)
    far = np.zeros((256, 256), ml_dtypes.bfloat16)
    for block in range(ROW):
        for e in range(2):
            for d in range(REACH):
                row = block * 16 + e * 8 + d
                near[row, 32 * d + 2 * block + e] = 1
                far[row, 32 * d + 2 * ((block - d - 1) % ROW) + e] = 1
    return np.stack([near, far])


def ahead_table():
    table = np.zeros((8, 256, 256), ml_dtypes.bfloat16)
    for g in range(8):
        for column in range(256):
            c = column % 32 + 2 * (column // 32 + 1)
            table[g, c if c < 32 else 128 + 16 * g + c - 32, column] = 1
    return table


def swap_bits(tiles, bits):
    lane = lax.broadcasted_iota(jnp.int32, tiles[0].shape, 1)
    tiles = list(tiles)
    for bit, shift in bits:
        low_half = (lane & shift) == 0
        for low in range(len(tiles)):
            if low & bit:
                continue
            a, b = tiles[low], tiles[low | bit]
            tiles[low] = jnp.where(low_half, a, pltpu.roll(b, shift, 1))
            tiles[low | bit] = jnp.where(low_half, pltpu.roll(a, 128 - shift, 1), b)
    return tiles


WAVES = (1, 7, 4, 2, 6, 3, 5, 0)
LOOK = 3
PITCH = 40
FPITCH = 136
CHUNKS = 4
CROWS = NBINS // CHUNKS
EROWS = CROWS // 8
TCH = 2
TW = LAG // TCH


def whole_kernel(
    raw_hbm, pair_ref, t_hbm, w_hbm, c_hbm, s_hbm, lc_hbm, ls_hbm, order_hbm, ahead_hbm, out_ref,
    raw_ref, t_ref, w_ref, c_ref, s_ref, lc_ref, ls_ref, order_ref, ahead_ref,
    stage, quarters, swapped, sent, landed, wide, first, spec_re, spec_im, white, edge_out, edge_in,
    cross_re, cross_im, present, near_out, wrap_out, wrap_in, far_out, near_in, far_in,
    load_sem, a_send, a_recv, x_send, x_recv, e_send, e_recv, n_send, n_recv, f_send, f_recv, w_send, w_recv,
):
    me, worker = lax.axis_index("blk"), lax.axis_index("pair")
    row, place = me // ROW, me % ROW
    behind = lax.rem(row + NROW - 1, NROW) * ROW + place
    ahead = lax.rem(row + 1, NROW) * ROW + place

    loads = [
        pltpu.make_async_copy(source, target, load_sem.at[k])
        for k, (source, target) in enumerate(
            (
                (raw_hbm, raw_ref), (t_hbm, t_ref), (w_hbm, w_ref), (c_hbm, c_ref), (s_hbm, s_ref),
                (ahead_hbm, ahead_ref), (lc_hbm, lc_ref), (ls_hbm, ls_ref), (order_hbm, order_ref),
            )
        )
    ]
    loads[0].start()

    def remote(source, target, send, recv, blk, pair):
        return pltpu.make_async_remote_copy(
            src_ref=source, dst_ref=target, send_sem=send, recv_sem=recv, device_id=(blk, pair), device_id_type=MESH
        )

    barrier = pltpu.get_barrier_semaphore()

    def greet(step, carry):
        pl.semaphore_signal(
            barrier, inc=1, device_id=(lax.rem(me + step, SPLIT), worker), device_id_type=MESH
        )
        return carry

    for step in range(1, PAIR):
        pl.semaphore_signal(
            barrier, inc=1, device_id=(me, lax.rem(worker + step, PAIR)), device_id_type=MESH
        )
    lax.fori_loop(1, SPLIT, greet, 0)
    loads[0].wait()

    def spread(to_row):
        for half in range(2):
            rows = pl.ds(16 * half, 16)
            tiles = []
            for block in range(ROW):
                at = pl.multiple_of(to_row * 2048 + block * 128, 128)
                tiles.append(raw_ref[0, rows, pl.ds(at, 128)].astype(f32))
            tiles = swap_bits(tiles, [(1, 2), (2, 4), (4, 8), (8, 16)])
            for block in range(ROW):
                stage[block, rows, :] = tiles[block].astype(bf16)

    def quarter(to_row):
        def some(index, carry):
            parts = []
            for k in range(2):
                block = stage[index * 2 + k].astype(f32)
                tiles = [block[8 * q : 8 * q + 8] for q in range(4)]
                parts.append(swap_bits(tiles, [(1, 32), (2, 64)]))
            at = pl.ds(pl.multiple_of(index * 16, 16), 16)
            for w in range(PAIR):
                quarters[w, to_row, at, :] = jnp.concatenate([parts[0][w], parts[1][w]], 0).astype(bf16)
            return carry

        lax.fori_loop(0, 8, some, 0, unroll=4)

    def prepare(wave):
        to_row = lax.rem(row + WAVES[wave], NROW)
        spread(to_row)
        quarter(to_row)

    def swap_workers(wave):
        to_row = lax.rem(row + WAVES[wave], NROW)
        for step in range(1, PAIR):
            there = lax.rem(worker + step, PAIR)
            remote(
                quarters.at[there, to_row], swapped.at[worker, to_row], x_send, x_recv.at[wave], me, there
            ).start()
        swapped[worker, to_row] = quarters[worker, to_row]

    def issue(wave):
        to_row = lax.rem(row + WAVES[wave], NROW)
        part = swapped.at[pl.ds(0, PAIR - 1), 0]
        remote(part, part, x_send, x_recv.at[wave], me, lax.rem(worker + 1, PAIR)).wait_recv()

        def join(index, carry):
            at = pl.ds(pl.multiple_of(index * 16, 16), 16)
            parts = [swapped[w, to_row, at, :].astype(f32) for w in range(PAIR)]
            for k in range(2):
                whole = jnp.concatenate([part[8 * k : 8 * k + 8] for part in parts], 0)
                sent[to_row * ROW + index * 2 + k] = whole.astype(bf16)
            return carry

        lax.fori_loop(0, 8, join, 0, unroll=4)

        def send(step, carry):
            shift = (step * 9) % 16
            chip = lax.rem(place // 2 + shift // 2, 8)
            core = lax.rem(place % 2 + shift % 2, 2)
            there = to_row * ROW + chip * 2 + core
            remote(sent.at[there], landed.at[me], a_send, a_recv.at[wave], there, worker).start()
            return carry

        lax.fori_loop(1, 16, send, 0)
        if WAVES[wave]:
            there = to_row * ROW + place
            remote(sent.at[there], landed.at[me], a_send, a_recv.at[wave], there, worker).start()
        else:
            landed[me] = sent[me]

    prepare(0)
    pl.semaphore_wait(barrier, SPLIT - 1 + PAIR - 1)
    swap_workers(0)
    for wave in range(1, NROW + LOOK):
        if wave < NROW:
            prepare(wave)
            swap_workers(wave)
        if wave >= LOOK:
            issue(wave - LOOK)
        if wave == LOOK:
            for load in loads[1:]:
                load.start()

    index = lax.broadcasted_iota(jnp.int32, (256, 768), 0)
    block, step = index // 16, index % REACH + 1
    for k, leading in enumerate((row * ROW + block, row * ROW + (block - step + ROW) % ROW)):
        found = (pair_ref[0:1, :] == leading) & (pair_ref[1:2, :] == leading + step)
        listed = jnp.max(jnp.where(found, 1.0, 0.0), axis=1, keepdims=True)
        present[k] = jnp.broadcast_to(listed, (256, 128))

    for load in loads[1:]:
        load.wait()
    for wave, distance in enumerate(WAVES):
        count = 15 if distance == 0 else 16
        remote(
            sent.at[pl.ds(0, count)], landed.at[pl.ds(0, count)], a_send, a_recv.at[wave], ahead, worker
        ).wait_recv()
        from_row = lax.rem(row + NROW - distance, NROW)

        def widen(index, carry, from_row=from_row):
            source = from_row * ROW + index
            wide[pl.ds(pl.multiple_of(source * PITCH, 8), 32), :] = landed[source].astype(f32)
            return carry

        lax.fori_loop(0, ROW, widen, 0, unroll=4)
    table = t_ref[...]

    def transform(index, carry):
        pair = [wide[pl.ds(index * 2 + k, 128, stride=PITCH), :].astype(bf16) for k in range(2)]
        got = jnp.dot(table, jnp.concatenate(pair, 1), preferred_element_type=f32)
        for k in range(2):
            first[index * 2 + k, pl.ds(0, 128)] = got[:, 128 * k : 128 * k + 128]
        return carry

    lax.fori_loop(0, 16, transform, 0, unroll=8)
    flat = first.reshape(32 * FPITCH, 128)

    def bands(slot, power):
        a = flat[pl.ds(slot, 32, stride=FPITCH), :]
        b = flat[pl.ds(slot + HALF, 32, stride=FPITCH), :]
        both = jnp.concatenate([a, b], 0)
        high = both.astype(bf16)
        low = (both - high.astype(f32)).astype(bf16)
        got = jnp.dot(
            w_ref[slot], jnp.concatenate([high, low, high], 0), preferred_element_type=f32
        )
        part_re, part_im = got[:BINS], got[BINS:]
        cos, sin = c_ref[slot], s_ref[slot]
        re = part_re * cos + part_im * sin
        im = part_im * cos - part_re * sin
        re = re + pltpu.roll(re, 64, 1)
        im = im + pltpu.roll(im, 64, 1)
        re = re + pltpu.roll(re, 32, 1)
        im = im + pltpu.roll(im, 32, 1)
        at = pl.ds(pl.multiple_of(slot * BINS, 8), BINS)
        spec_re[at, :] = re
        spec_im[at, :] = im
        return power + re * re + im * im

    power = lax.fori_loop(0, HALF, bands, jnp.zeros((BINS, 128), f32), unroll=16)
    parity = lax.broadcasted_iota(jnp.int32, (BINS, 128), 0) % 2
    other = jnp.where(parity == 0, pltpu.roll(power, BINS - 1, 0), pltpu.roll(power, 1, 0))
    gain = lax.rsqrt((power + other) / SPLIT + EPSILON)
    gain = jnp.concatenate([gain, gain], 0)
    group = lax.broadcasted_iota(jnp.int32, (EROWS, 128), 1) // 16

    for chunk in range(CHUNKS):
        for k, spec in enumerate((spec_re, spec_im)):
            packed = None
            for g in range(8):
                at = pl.ds(CROWS * chunk + EROWS * g, EROWS)
                value = (spec[at, :] * gain).astype(bf16)
                white[k, at, :] = value
                value = value.astype(f32)
                value = pltpu.roll(value, 16, 1) if g % 2 else value
                packed = value if g == 0 else jnp.where(group == g, value, packed)
            edge_out[chunk, k] = packed.astype(bf16)
        remote(
            edge_out.at[chunk], edge_in.at[chunk], e_send.at[chunk], e_recv.at[chunk], behind, worker
        ).start()

    for chunk in range(CHUNKS):
        remote(
            edge_out.at[chunk], edge_in.at[chunk], e_send.at[chunk], e_recv.at[chunk], behind, worker
        ).wait()

        def cross(g, carry, chunk=chunk):
            at = pl.ds(pl.multiple_of(CROWS * chunk + EROWS * g, 16), EROWS)
            own = [white[k, at, :] for k in range(2)]
            both = [jnp.concatenate([own[k], edge_in[chunk, k]], 1) for k in range(2)]
            got = jnp.dot(
                jnp.concatenate(both, 0), ahead_ref[g], preferred_element_type=f32
            )
            a, f = own[0].astype(f32), own[1].astype(f32)
            for tile in range(2):
                columns = slice(128 * tile, 128 * tile + 128)
                e, h = got[:EROWS, columns], got[EROWS:, columns]
                cross_re[at, columns] = (a * e + f * h).astype(bf16)
                cross_im[at, columns] = (f * e - a * h).astype(bf16)
            return carry

        lax.fori_loop(0, 8, cross, 0, unroll=4)

    inv_root = 1.0 / math.sqrt(NBINS)
    offset = lax.broadcasted_iota(jnp.int32, (16, TW), 0) % REACH
    nt = (((1,), (1,)), ((), ()))
    for t in range(TCH):
        lags = pl.ds(TW * t, TW)
        even = jnp.dot(lc_ref[lags, :], cross_re[...], preferred_element_type=f32)
        odd = jnp.dot(ls_ref[lags, :], cross_im[...], preferred_element_type=f32)

        def ordered(k, half):
            half = (half * inv_root).astype(bf16)
            half = lax.dot_general(order_ref[k], half, nt, preferred_element_type=f32)
            listed = jnp.concatenate([present[k]] * (TW // 128), 1) > 0.5
            return jnp.where(listed, half, 0.0).astype(bf16)

        near_out[t] = ordered(0, even - odd).reshape(ROW, 16, TW)

        def send_near(step, carry, t=t):
            to = lax.rem(place + (step * 7) % 16, ROW)
            remote(
                near_out.at[t, to], near_in.at[t, place], n_send, n_recv.at[t], row * ROW + to, worker
            ).start()
            return carry

        lax.fori_loop(1, ROW, send_near, 0)
        far = ordered(1, even + odd)
        wrap_out[t] = far[: 16 * REACH]
        far_out[t] = far
        remote(wrap_out.at[t], wrap_in.at[t], w_send.at[t], w_recv.at[t], ahead, worker).start()

    for t in range(TCH):
        remote(wrap_out.at[t], wrap_in.at[t], w_send.at[t], w_recv.at[t], ahead, worker).wait()
        for block in range(REACH):
            at = pl.ds(16 * block, 16)
            far_out[t, at, :] = jnp.where(
                offset < block, far_out[t, at, :].astype(f32), wrap_in[t, at, :].astype(f32)
            ).astype(bf16)

        def send_far(step, carry, t=t):
            to = lax.rem(place + (step * 7) % 16, ROW)
            at = pl.ds(pl.multiple_of(to * 16, 16), 16)
            remote(
                far_out.at[t, at], far_in.at[t, place], f_send, f_recv.at[t], row * ROW + to, worker
            ).start()
            return carry

        lax.fori_loop(1, ROW, send_far, 0)

    for t in range(TCH):
        near_in[t, place] = near_out[t, place]
        far_in[t, place] = far_out[t, pl.ds(pl.multiple_of(place * 16, 16), 16), :]
    for t in range(TCH):
        for arrived, send, recv in ((near_in, n_send, n_recv), (far_in, f_send, f_recv)):
            most = arrived.at[t, pl.ds(0, ROW - 1)]
            remote(most, most, send, recv.at[t], ahead, worker).wait_recv()

        def store(r, carry, t=t):
            near, far = near_in[t, r].astype(f32), far_in[t, r].astype(f32)
            for e in range(2):
                both = jnp.concatenate([near[8 * e : 8 * e + 8], far[8 * e : 8 * e + 8]], 0)
                out_ref[2 * r + e, :, TW * t : TW * t + TW] = both.astype(bf16)
            return carry

        lax.fori_loop(0, ROW, store, 0, unroll=4)

    most = sent.at[pl.ds(0, SPLIT - 1)]
    remote(most, most, a_send, a_recv.at[0], ahead, worker).wait_send()
    most = quarters.at[pl.ds(0, PAIR - 1)]
    remote(most, most, x_send, x_recv.at[0], ahead, worker).wait_send()
    most = near_in.at[:, pl.ds(0, ROW - 1)]
    remote(most, most, n_send, n_recv.at[0], ahead, worker).wait_send()
    most = far_in.at[:, pl.ds(0, ROW - 1)]
    remote(most, most, f_send, f_recv.at[0], ahead, worker).wait_send()


def shards(raw, pair_list):
    weights, cos, sin = second_tables()
    lag_cos, lag_sin = lag_tables()
    tables = [first_table(), weights, cos, sin, lag_cos, lag_sin, order_tables(), ahead_table()]
    anywhere = pl.BlockSpec(memory_space=pl.ANY)
    vmem = pl.BlockSpec(memory_space=pltpu.VMEM)
    dma = pltpu.SemaphoreType.DMA
    halves = pl.pallas_call(
        whole_kernel,
        name="whole",
        out_shape=jax.ShapeDtypeStruct((32, 2 * REACH, LAG), bf16),
        in_specs=[anywhere, vmem] + [anywhere] * len(tables),
        out_specs=vmem,
        scratch_shapes=[
            pltpu.VMEM(raw.shape, bf16),
            *(pltpu.VMEM(table.shape, table.dtype) for table in tables),
            pltpu.VMEM((ROW, 32, 128), bf16),
            pltpu.VMEM((PAIR, NROW, 128, 128), bf16),
            pltpu.VMEM((PAIR, NROW, 128, 128), bf16),
            pltpu.VMEM((SPLIT, 32, 128), bf16),
            pltpu.VMEM((SPLIT, 32, 128), bf16),
            pltpu.VMEM((SPLIT * PITCH, 128), f32),
            pltpu.VMEM((32, FPITCH, 128), f32),
            pltpu.VMEM((NBINS, 128), f32),
            pltpu.VMEM((NBINS, 128), f32),
            pltpu.VMEM((2, NBINS, 128), bf16),
            pltpu.VMEM((CHUNKS, 2, EROWS, 128), bf16),
            pltpu.VMEM((CHUNKS, 2, EROWS, 128), bf16),
            pltpu.VMEM((NBINS, 256), bf16),
            pltpu.VMEM((NBINS, 256), bf16),
            pltpu.VMEM((2, 256, 128), f32),
            pltpu.VMEM((TCH, ROW, 16, TW), bf16),
            pltpu.VMEM((TCH, 16 * REACH, TW), bf16),
            pltpu.VMEM((TCH, 16 * REACH, TW), bf16),
            pltpu.VMEM((TCH, 16 * ROW, TW), bf16),
            pltpu.VMEM((TCH, ROW, 16, TW), bf16),
            pltpu.VMEM((TCH, ROW, 16, TW), bf16),
            dma((9,)),
            dma,
            dma((len(WAVES),)),
            dma,
            dma((len(WAVES),)),
            dma((CHUNKS,)),
            dma((CHUNKS,)),
            dma,
            dma((TCH,)),
            dma,
            dma((TCH,)),
            dma((TCH,)),
            dma((TCH,)),
        ],
        compiler_params=pltpu.CompilerParams(
            collective_id=0, has_side_effects=True, vmem_limit_bytes=VMEM
        ),
    )(raw, pair_list.T, *(jnp.asarray(table) for table in tables))
    return halves.astype(f32)[None]


def solution(mesh):
    return jax.shard_map(
        shards,
        mesh=mesh,
        in_specs=(P("blk", "pair", None), P()),
        out_specs=P("blk", "pair", None, None),
        check_vma=False,
    )
```
